512 devices in a mesh: side: 4 (over z_lo, core), grp: 8 (over y), tp: 16 (over x, z_hi).
Axes of the slice: x: 4, y: 8, z: 8 (z_hi: 4, z_lo: 2; z = z_hi * 2 + z_lo), core: 2. Of those that a mesh axis runs over, the one named last changes fastest.
Arguments:
- resident_kv: bfloat16 [1024, 256, 2048], P(('side', 'grp', 'tp')), may hold values from -32 to 32
- resident_query: bfloat16 [1024, 16384], P(('side', 'grp'), 'tp'), may hold values from -32 to 32
- resident_new: bfloat16 [1024, 2048], P(('side', 'grp', 'tp')), may hold values from -9 to 9
- lengths: int32 [1024], P(('side', 'grp', 'tp')), may hold values from 2 to 256
- fresh_kv: bfloat16 [4096, 16, 2048], P(('side', 'grp', 'tp')), may hold values from -32 to 32
- handed_query: bfloat16 [32, 16, 8, 2, 16384], P(('side', 'grp'), None, None, None, 'tp'), may hold values from -32 to 32
- fresh_new: bfloat16 [4096, 2048], P(('side', 'grp', 'tp')), may hold values from -9 to 9
- matching: int32 [4096, 1], P(('side', 'grp', 'tp')), may hold values from 0 to 7; in each aligned block of 8 rows (0 to 7, 8 to 15, ...) at most 2 rows name the same one
Outputs:
- resident_out: bfloat16 [1024, 16384], P(('side', 'grp'), 'tp')
- handed_out: bfloat16 [32, 16, 8, 2, 16384], P(('side', 'grp'), None, None, None, 'tp')
- handed_cache_out: bfloat16 [32, 16, 8, 2, 16, 2048], P(('side', 'grp'), 'tp')
The draws below stay inside these ranges and needn't reach their ends.
Inputs may be any that keep to these rules, and one draw needn't show every extreme that they name: `matching`: within each device's 8 requests no decode group is named more than 2 times.
All inputs are finite; a program needn't handle non-finite values.
Results may differ from the reference program's by a relative error of at most 0.0026.
Values may be sent and summed in bfloat16 or wider, within the bound.
A program may use at most 64 MiB of HBM per device.

```python
import math
import jax
import jax.numpy as jnp
import numpy as np
from jax import lax

QH = 128
KVH = 8
HD = 128
LR = 256
REQ_DEV = 8
LP = 16
MOST = 2
GROUPS = 32
ROWS_ALL = 1024
REQS_ALL = 4096
N_SIDE = 4
N_GRP = 8
N_TP = 16


def draw_resident_kv(key, part):
    key = jax.random.fold_in(key, 11)
    shape = (ROWS_ALL, LR, 2 * KVH * HD)
    noise = jnp.clip(jax.random.normal(key, shape, dtype=jnp.float32), -6.0, 6.0)
    return noise.astype(jnp.bfloat16)


def draw_resident_query(key, part):
    key = jax.random.fold_in(key, 12)
    shape = (ROWS_ALL, QH * HD)
    noise = jnp.clip(2.5 * jax.random.normal(key, shape, dtype=jnp.float32), -15.0, 15.0)
    return noise.astype(jnp.bfloat16)


def draw_fresh_kv(key, part):
    key = jax.random.fold_in(key, 13)
    shape = (REQS_ALL, LP, 2 * KVH * HD)
    noise = jnp.clip(jax.random.normal(key, shape, dtype=jnp.float32), -6.0, 6.0)
    return noise.astype(jnp.bfloat16)


def draw_handed_query(key, part):
    key = jax.random.fold_in(key, 14)
    count = GROUPS * N_TP * N_GRP * MOST
    shape = (count, QH * HD)
    planted = jnp.clip(2.5 * jax.random.normal(key, shape, dtype=jnp.float32), -15.0, 15.0)
    return planted.reshape(GROUPS, N_TP, N_GRP, MOST, QH * HD).astype(jnp.bfloat16)


def draw_lengths(key, part):
    key = jax.random.fold_in(key, 15)
    first_key, second_key = jax.random.split(key)
    spread = jax.random.randint(first_key, (ROWS_ALL,), 2, LR + 1, dtype=jnp.int32)
    where_full = jax.random.randint(second_key, (), 0, ROWS_ALL, dtype=jnp.int32)
    return jnp.where(jnp.arange(ROWS_ALL, dtype=jnp.int32) == where_full, jnp.int32(LR), spread)


def block_levels(key, extent, cuts, low, largest):
    def one(position, shards_of):
        steps = jax.random.uniform(jax.random.fold_in(jax.random.fold_in(key, 6), position), (shards_of,), jnp.float32, low / len(cuts), largest / len(cuts))
        return jnp.repeat(jnp.exp(steps), extent[position] // shards_of).reshape((-1,) + (1,) * (len(extent) - position - 1))

    level = one(*cuts[0])
    for cut in cuts[1:]:
        level = level * one(*cut)
    return level


def routed_block(rng, own, number, rows, number_of, top, reach, skew):
    sequence = jax.random.permutation(rng, number_of)
    packed, usual = shares(number_of, rows * top, reach, skew, True), shares(number_of, rows * top, reach, skew, False)
    places = jnp.arange(number_of)

    def named(tallies, rotation):
        used = int((tallies > 0).sum())
        fixed = max(1, used // 4)
        moved = fixed + (places - fixed + rotation * (used - fixed)) % max(1, number_of - fixed)
        return jnp.zeros((number_of,), jnp.int32).at[sequence[jnp.where(places < fixed, places, moved)]].set(jnp.asarray(tallies, jnp.int32))

    tallies = jnp.where(number % 4 == 0, named(packed, number // 4), named(usual, number - number // 4 - 1))
    mixed = jax.random.permutation(jax.random.fold_in(own, 3), number_of)
    donor, receiver = mixed[0:number_of // 2 * 2:2], mixed[1:number_of // 2 * 2:2]
    room = jnp.minimum(tallies[donor] - 1, reach - tallies[receiver]) // 2
    room = jnp.where((donor == sequence[0]) | (receiver == sequence[0]) | (tallies[receiver] == 0), 0, jnp.maximum(room, 0))
    moved = jax.random.randint(jax.random.fold_in(own, 4), (number_of // 2,), 0, 1 << 20) % (room + 1)
    tallies = tallies.at[donor].add(-moved).at[receiver].add(moved)
    labels = jnp.searchsorted(jnp.cumsum(tallies), jnp.arange(rows * top), side="right").astype(jnp.int32)
    table = labels.reshape(top, rows).T
    table = table[jax.random.permutation(jax.random.fold_in(own, 1), rows)]
    rotation = jax.random.randint(jax.random.fold_in(own, 2), (rows, 1), 0, top)
    return jnp.take_along_axis(table, (jnp.arange(top)[None, :] + rotation) % top, axis=1)


def shares(amount, total, reach, lean, full):
    portions = [(1 << 20) // math.isqrt(standing ** lean) + 1 for standing in range(1, amount + 1)]
    largest = reach if full else min(reach, max(-(-total // amount), total * portions[0] // sum(portions)))
    least = 1 if total - largest >= amount - 1 else 0
    holding, spare = [largest] + [least] * (amount - 1), total - largest - least * (amount - 1)
    while spare > 0:
        candidates = [i for i in range(1, amount) if holding[i] < largest] or [i for i in range(1, amount) if holding[i] < reach]
        whole, remaining = sum([portions[i] for i in candidates]), spare
        for i in candidates:
            extra = min(reach - holding[i], max(1, remaining * portions[i] // whole), spare)
            holding[i] = holding[i] + extra
            spare = spare - extra
    return np.array(holding)


def normal_values(own_key, extent, deviation, limit, cuts=(), held_as=jnp.bfloat16):
    values = deviation * jax.random.normal(own_key, extent, jnp.float32)
    if cuts:
        values = values * block_levels(own_key, extent, cuts, -0.22, 0.18)
    return jnp.clip(values, -limit, limit).astype(held_as)


def setup_inputs(seed: int = 0) -> dict:
    key_list = jax.random.split(jax.random.key(seed), 9)
    resident_kv = draw_resident_kv(jax.random.fold_in(key_list[8], 71), 0)
    resident_query = draw_resident_query(jax.random.fold_in(key_list[8], 71), 0)
    resident_new = normal_values(key_list[2], (ROWS_ALL, 2 * KVH * HD), 1.5, 9.0, ((0, 512),))
    lengths = draw_lengths(jax.random.fold_in(key_list[8], 71), 0)
    fresh_kv = draw_fresh_kv(jax.random.fold_in(key_list[8], 71), 0)
    handed_query = draw_handed_query(jax.random.fold_in(key_list[8], 71), 0)
    fresh_new = normal_values(key_list[6], (REQS_ALL, 2 * KVH * HD), 1.5, 9.0, ((0, 512),))
    matching_keys = jax.random.split(jax.random.fold_in(key_list[7], 1), REQS_ALL // REQ_DEV)
    matching_turns = jax.random.permutation(jax.random.fold_in(key_list[7], 3), REQS_ALL // REQ_DEV)
    matching = jax.vmap(lambda own, number: routed_block(jax.random.fold_in(key_list[7], 2), own, number, REQ_DEV, N_GRP, 1, MOST, 2))(matching_keys, matching_turns).reshape((REQS_ALL, 1))
    return dict(resident_kv=resident_kv, resident_query=resident_query, resident_new=resident_new, lengths=lengths, fresh_kv=fresh_kv, handed_query=handed_query, fresh_new=fresh_new, matching=matching)


NEG_FILL = -1e+30

def attend_row(query, cache, valid, new_pair):
    group = QH // KVH
    scale = 1.0 / math.sqrt(HD)
    length = cache.shape[0]
    heads = query.astype(jnp.float32).reshape(KVH, group, HD)
    keys = cache[:, :KVH * HD].astype(jnp.float32).reshape(length, KVH, HD)
    values = cache[:, KVH * HD:].astype(jnp.float32).reshape(length, KVH, HD)
    scores = jnp.einsum('hgd,lhd->hgl', heads, keys) * scale
    scores = jnp.where(valid[None, None, :], scores, NEG_FILL)
    new_keys = new_pair[:KVH * HD].astype(jnp.float32).reshape(KVH, HD)
    new_values = new_pair[KVH * HD:].astype(jnp.float32).reshape(KVH, HD)
    new_score = jnp.einsum('hgd,hd->hg', heads, new_keys) * scale
    top = jnp.maximum(lax.optimization_barrier(jnp.max(scores, axis=-1)), new_score)
    probs = jnp.where(valid[None, None, :], jnp.exp(scores - top[..., None]), 0.0)
    new_prob = jnp.exp(new_score - top)
    total = lax.optimization_barrier(jnp.sum(probs, axis=-1)) + new_prob
    weights = lax.optimization_barrier(probs.astype(jnp.bfloat16)).astype(jnp.float32)
    new_weight = lax.optimization_barrier(new_prob.astype(jnp.bfloat16)).astype(jnp.float32)
    numer = jnp.einsum('hgl,lhd->hgd', weights, values) + new_weight[..., None] * new_values[:, None, :]
    return (numer / total[..., None]).reshape(QH * HD).astype(jnp.bfloat16)

def reference(resident_kv, resident_query, resident_new, lengths, fresh_kv, handed_query, fresh_new, matching):
    positions = jnp.arange(LR, dtype=jnp.int32)

    def resident_row(items):
        query, cache, length, pair = items
        return attend_row(query, cache, positions < length, pair)
    resident_out = lax.map(resident_row, (resident_query, resident_kv, lengths, resident_new))
    devices = N_SIDE * N_GRP * N_TP
    target = matching[:, 0].reshape(devices, REQ_DEV)
    order = jnp.arange(REQ_DEV, dtype=jnp.int32)
    earlier = (target[:, :, None] == target[:, None, :]) & (order[None, :, None] < order[None, None, :])
    rank = lax.optimization_barrier(jnp.sum(earlier.astype(jnp.int32), axis=1))
    device = jnp.arange(devices, dtype=jnp.int32)
    source_side = device // (N_GRP * N_TP)
    source_grp = device // N_TP % N_GRP
    source_tp = device % N_TP
    dest_group = ((source_side + N_SIDE // 2) % N_SIDE * N_GRP)[:, None] + target
    grp_index = jnp.broadcast_to(source_grp[:, None], (devices, REQ_DEV))
    tp_index = jnp.broadcast_to(source_tp[:, None], (devices, REQ_DEV))
    dest_flat = dest_group.reshape(-1).astype(jnp.int32)
    tp_flat = tp_index.reshape(-1).astype(jnp.int32)
    grp_flat = grp_index.reshape(-1).astype(jnp.int32)
    rank_flat = rank.reshape(-1).astype(jnp.int32)
    queries = handed_query[dest_flat, tp_flat, grp_flat, rank_flat]
    everything = jnp.ones((LP,), dtype=bool)

    def fresh_row(items):
        query, cache, pair = items
        return attend_row(query, cache, everything, pair)
    fresh_out = lax.map(fresh_row, (queries, fresh_kv, fresh_new))
    handed_out = jnp.zeros((N_SIDE * N_GRP, N_TP, N_GRP, MOST, QH * HD), jnp.bfloat16)
    handed_out = handed_out.at[dest_flat, tp_flat, grp_flat, rank_flat].set(fresh_out)
    handed_cache_out = jnp.zeros((N_SIDE * N_GRP, N_TP, N_GRP, MOST, LP, 2 * KVH * HD), jnp.bfloat16)
    handed_cache_out = handed_cache_out.at[dest_flat, tp_flat, grp_flat, rank_flat].set(fresh_kv.astype(jnp.bfloat16))
    return (resident_out, handed_out, handed_cache_out)
```

```python
import functools
import math

import jax
import jax.numpy as jnp
from jax import lax
from jax.experimental import pallas as pl
from jax.experimental.pallas import tpu as pltpu
from jax.sharding import PartitionSpec as P

MESH = pl.DeviceIdType.MESH
BF = jnp.bfloat16
F32 = jnp.float32
HD = 128
KVH = 8
N_GRP = 8
N_TP = 16
NEG_FILL = -1e30
SCALE = 1.0 / math.sqrt(HD)
HC = 2
NCH = KVH // HC
W = HC * HD


def iota(shape, dim):
    return lax.broadcasted_iota(jnp.int32, shape, dim)


def attend(q, k, v, new_k, new_v, valid):
    s = lax.dot_general(q, k, (((1,), (1,)), ((), ())), preferred_element_type=F32) * SCALE
    s = jnp.where(valid, s, NEG_FILL)
    sn = jnp.sum(q.astype(F32) * new_k, axis=-1, keepdims=True) * SCALE
    top = jnp.maximum(jnp.max(s, axis=-1, keepdims=True), sn)
    p = jnp.exp(s - top)
    pn = jnp.exp(sn - top)
    total = jnp.sum(p, axis=-1, keepdims=True) + pn
    numer = jnp.dot(p.astype(BF), v, preferred_element_type=F32)
    numer = numer + pn.astype(BF).astype(F32) * new_v
    return (numer / total).astype(BF)


def kernel(
    kv_any, rq_ref, rn_ref, len_ref, fkv_any, hq_any, fn_ref, mt_ref,
    ro_ref, ho_any, hc_any,
    rkv, rqf, rqt, rqs, rqb, ros, rob, rof, rot, place_s, place_r, new_s, new_r,
    npk, nb, land, sel, pk, kvb, qb, osd,
    loc, cps, pls, plr, nws, nwr, s1s, s1r, nys, nyr, s2s, s2r, rqss, rqr, qs, qr, rosm, ror, os_, orr,
):
    side = lax.axis_index("side")
    g = lax.axis_index("grp")
    i = lax.axis_index("tp")
    sp = (side + 2) % 4
    c0 = i // (2 * HC)

    def remote(src, dst, ss, rs, **dev):
        return pltpu.make_async_remote_copy(
            src_ref=src, dst_ref=dst, send_sem=ss, recv_sem=rs, device_id=dev, device_id_type=MESH
        )

    def over(n, f):
        def body(k, _):
            f(k)
            return 0

        lax.fori_loop(0, n, body, 0)

    def d_stage1(c, part):
        cols = pl.ds(pl.multiple_of(part * KVH * HD + c * W, 128), W)
        return remote(
            fkv_any.at[:, :, cols], land.at[c, :, :, pl.ds(part * W, W)],
            s1s.at[c, part], s1r.at[c, part], side=sp,
        )

    def d_place():
        return remote(place_s, place_r, pls, plr, side=sp)

    def d_new():
        return remote(new_s, new_r, nws, nwr, side=sp)

    def d_new_y(d, me):
        return remote(npk.at[d], nb.at[me], nys.at[d], nyr.at[me], grp=d)

    def d_kv_y(c, d, me):
        return remote(pk.at[c, d], kvb.at[c, me], s2s.at[c, d], s2r.at[c, me], grp=d)

    def d_rq(t, me):
        return remote(rqs.at[t], rqb.at[me], rqss.at[t], rqr.at[me], tp=t)

    def d_q(t, me):
        return remote(hq_any.at[t], qb.at[me], qs.at[t], qr.at[me], tp=t)

    def d_ro(t, me):
        return remote(ros.at[t], rob.at[me], rosm.at[t], ror.at[me], tp=t)

    def d_out(t, me):
        return remote(osd.at[t], ho_any.at[me], os_.at[t], orr.at[me], tp=t)

    def l_kv():
        return pltpu.make_async_copy(kv_any, rkv, loc.at[0])

    def l_q():
        return pltpu.make_async_copy(hq_any.at[i], qb.at[i], loc.at[1])

    def l_out():
        return pltpu.make_async_copy(osd.at[i], ho_any.at[i], loc.at[2])

    def l_cache(c, part):
        cols = pl.ds(pl.multiple_of(part * KVH * HD + c * W, 128), W)
        return pltpu.make_async_copy(
            kvb.at[c, :, :, pl.ds(part * W, W)], hc_any.at[:, :, cols], cps.at[c, part]
        )

    def tp_peer(k):
        return (i + N_TP - 1 - k) % N_TP

    def grp_peer(k):
        return (g + 1 + k) % N_GRP

    l_kv().start()
    l_q().start()
    barrier = pltpu.get_barrier_semaphore()
    pl.semaphore_signal(barrier, inc=1, device_id={"side": sp}, device_id_type=MESH)
    over(N_GRP - 1, lambda k: pl.semaphore_signal(
        barrier, inc=1, device_id={"grp": grp_peer(k)}, device_id_type=MESH))
    over(N_TP - 1, lambda k: pl.semaphore_signal(
        barrier, inc=1, device_id={"tp": tp_peer(k)}, device_id_type=MESH))

    m = jnp.broadcast_to(mt_ref[...], (8, 128))
    row, lane = iota((8, 128), 0), iota((8, 128), 1)

    def places(req):
        mrow = jnp.sum(jnp.where(row == req, m, 0), axis=0, keepdims=True)
        mine = jnp.broadcast_to(mrow, (8, 128))
        rank = jnp.sum(jnp.where((m == mine) & (row < req), 1, 0), axis=0, keepdims=True)
        return jnp.broadcast_to(mrow * 2 + rank, (8, 128))

    wide = places(lane // 16) * 16 + lane % 16
    narrow = jnp.where(lane < 8, places(lane), -1)
    place_s[...] = jnp.where(row < 4, wide, narrow)
    new_s[...] = jnp.concatenate([fn_ref[...], jnp.zeros((8, 2 * KVH * HD), BF)], axis=0)
    for j in range(8):
        rqf[32 * j:32 * j + 32] = rq_ref[:, 128 * j:128 * j + 128].astype(F32)
    for j in range(8):
        for r in range(2):
            rqt[pl.ds(2 * j + r, 16, stride=16), :] = rqf[pl.ds(32 * j + r, 16, stride=2), :]
    rqs[...] = rqt[...].astype(BF).reshape(16, 16, 128)
    rqb[i] = rqs[i]

    pl.semaphore_wait(barrier, N_TP + N_GRP - 1)

    d_place().start()

    def start1(t):
        c = (c0 + t) % NCH
        d_stage1(c, 0).start()
        d_stage1(c, 1).start()

    over(NCH, start1)
    d_new().start()
    over(N_TP - 1, lambda k: d_rq(tp_peer(k), i).start())
    over(N_TP - 1, lambda k: d_q(tp_peer(k), i).start())

    d_place().wait_recv()
    sel[...] = jnp.where(iota((256, 128), 0) == place_r[0:1, :], 1.0, 0.0).astype(BF)
    sel16 = jnp.where(iota((16, 16), 0) == place_r[4:5, 0:16], 1.0, 0.0).astype(BF)

    def pack(t):
        c = (c0 + t) % NCH
        d_stage1(c, 0).wait_recv()
        d_stage1(c, 1).wait_recv()
        x = land[c].reshape(128, 2 * W)
        y = jnp.dot(sel[...], x, preferred_element_type=F32).astype(BF)
        pk[c] = y.reshape(8, 32, 2 * W)
        over(N_GRP - 1, lambda k: d_kv_y(c, grp_peer(k), g).start())
        kvb[c, g] = pk[c, g]

    over(NCH, pack)

    d_new().wait_recv()
    for c in range(16):
        cols = slice(128 * c, 128 * c + 128)
        y = jnp.dot(sel16, new_r[:, cols], preferred_element_type=F32).astype(BF)
        npk[:, :, cols] = y.reshape(8, 2, 128)
    over(N_GRP - 1, lambda k: d_new_y(grp_peer(k), g).start())
    nb[g] = npk[g]

    l_kv().wait()
    over(N_TP - 1, lambda k: d_rq(tp_peer(k), tp_peer(k)).wait_recv())
    rrow, rcol = iota((32, 512), 0) % 2, iota((32, 512), 1)
    length = jnp.where(rrow == 0, len_ref[0], len_ref[1])
    rvalid = (rcol // 256 == rrow) & (rcol % 256 < length)
    first = iota((32, 128), 0) % 2 == 0

    def resident(h):
        q = jnp.concatenate([rqb[2 * h], rqb[2 * h + 1]], axis=0)
        kcols = pl.ds(pl.multiple_of(h * 128, 128), 128)
        vcols = pl.ds(pl.multiple_of(KVH * HD + h * 128, 128), 128)
        k = rkv[:, :, kcols].reshape(512, 128)
        v = rkv[:, :, vcols].reshape(512, 128)
        nk = rn_ref[:, kcols].astype(F32)
        nv = rn_ref[:, vcols].astype(F32)
        o = attend(
            q, k, v, jnp.where(first, nk[0:1], nk[1:2]), jnp.where(first, nv[0:1], nv[1:2]), rvalid
        )
        ros[2 * h] = o[0:16]
        ros[2 * h + 1] = o[16:32]

    over(KVH, resident)
    over(N_TP - 1, lambda k: d_ro(tp_peer(k), i).start())
    rob[i] = ros[i]

    over(N_GRP - 1, lambda k: d_new_y(grp_peer(k), grp_peer(k)).wait_recv())
    l_q().wait()
    hvalid = iota((256, 256), 0) % 16 == iota((256, 256), 1) // 16

    def handed(t):
        c = (c0 + t) % NCH
        over(N_GRP - 1, lambda k: d_kv_y(c, grp_peer(k), grp_peer(k)).wait_recv())
        l_cache(c, 0).start()
        l_cache(c, 1).start()
        for u in range(HC):
            h = c * HC + u
            for t2 in range(2):
                @pl.when(2 * h + t2 != i)
                def _():
                    d_q(2 * h + t2, 2 * h + t2).wait_recv()
            q = jnp.concatenate(
                [
                    qb[2 * h + t2, :, :, 128 * j:128 * j + 128].reshape(16, 128)
                    for t2 in range(2) for j in range(8)
                ],
                axis=0,
            )
            k = kvb[c, :, :, 128 * u:128 * u + 128].reshape(256, 128)
            v = kvb[c, :, :, W + 128 * u:W + 128 * u + 128].reshape(256, 128)
            kcols = pl.ds(pl.multiple_of(h * 128, 128), 128)
            vcols = pl.ds(pl.multiple_of(KVH * HD + h * 128, 128), 128)
            nk = nb[:, :, kcols].reshape(16, 128).astype(F32)
            nv = nb[:, :, vcols].reshape(16, 128).astype(F32)
            o = attend(q, k, v, jnp.tile(nk, (16, 1)), jnp.tile(nv, (16, 1)), hvalid)
            for t2 in range(2):
                for j in range(8):
                    at = 16 * (8 * t2 + j)
                    osd[2 * h + t2, :, :, 128 * j:128 * j + 128] = o[at:at + 16].reshape(8, 2, 128)
            for t2 in range(2):
                @pl.when(2 * h + t2 != i)
                def _():
                    d_out(2 * h + t2, i).start()

    over(NCH, handed)
    l_out().start()

    over(N_TP - 1, lambda k: d_ro(tp_peer(k), tp_peer(k)).wait_recv())
    rof[...] = rob[...].reshape(256, 128).astype(F32)
    for j in range(8):
        for r in range(2):
            rot[pl.ds(32 * j + r, 16, stride=2), :] = rof[pl.ds(2 * j + r, 16, stride=16), :]
    for j in range(8):
        ro_ref[:, 128 * j:128 * j + 128] = rot[32 * j:32 * j + 32].astype(BF)

    d_place().wait_send()
    d_new().wait_send()

    def end_chunk(c):
        for part in range(2):
            d_stage1(c, part).wait_send()
            l_cache(c, part).wait()
        over(N_GRP - 1, lambda k: d_kv_y(c, grp_peer(k), g).wait_send())

    over(NCH, end_chunk)
    over(N_GRP - 1, lambda k: d_new_y(grp_peer(k), g).wait_send())

    def end_tp(k):
        t = tp_peer(k)
        d_rq(t, i).wait_send()
        d_q(t, i).wait_send()
        d_ro(t, i).wait_send()
        d_out(t, i).wait_send()
        d_out(t, t).wait_recv()

    over(N_TP - 1, end_tp)
    l_out().wait()


def body(
    resident_kv, resident_query, resident_new, lengths, fresh_kv, handed_query, fresh_new, matching
):
    vm = pl.BlockSpec(memory_space=pltpu.VMEM)
    sm = pl.BlockSpec(memory_space=pltpu.SMEM)
    anys = pl.BlockSpec(memory_space=pl.ANY)
    dma = pltpu.SemaphoreType.DMA
    ro, ho, hc = pl.pallas_call(
        kernel,
        out_shape=(
            jax.ShapeDtypeStruct((32, 1024), BF),
            jax.ShapeDtypeStruct((16, 8, 2, 1024), BF),
            jax.ShapeDtypeStruct((8, 32, 2048), BF),
        ),
        in_specs=[anys, vm, vm, sm, anys, anys, vm, vm],
        out_specs=(vm, anys, anys),
        scratch_shapes=[
            pltpu.VMEM((2, 256, 2048), BF),
            pltpu.VMEM((256, 128), F32),
            pltpu.VMEM((256, 128), F32),
            pltpu.VMEM((16, 16, 128), BF),
            pltpu.VMEM((16, 16, 128), BF),
            pltpu.VMEM((16, 16, 128), BF),
            pltpu.VMEM((16, 16, 128), BF),
            pltpu.VMEM((256, 128), F32),
            pltpu.VMEM((256, 128), F32),
            pltpu.VMEM((8, 128), jnp.int32),
            pltpu.VMEM((8, 128), jnp.int32),
            pltpu.VMEM((16, 2048), BF),
            pltpu.VMEM((16, 2048), BF),
            pltpu.VMEM((8, 2, 2048), BF),
            pltpu.VMEM((8, 2, 2048), BF),
            pltpu.VMEM((NCH, 8, 16, 2 * W), BF),
            pltpu.VMEM((256, 128), BF),
            pltpu.VMEM((NCH, 8, 32, 2 * W), BF),
            pltpu.VMEM((NCH, 8, 32, 2 * W), BF),
            pltpu.VMEM((16, 8, 2, 1024), BF),
            pltpu.VMEM((16, 8, 2, 1024), BF),
            dma((3,)), dma((NCH, 2)),
            dma, dma, dma, dma,
            dma((NCH, 2)), dma((NCH, 2)),
            dma((8,)), dma((8,)),
            dma((NCH, 8)), dma((NCH, 8)),
            dma((16,)), dma((16,)), dma((16,)), dma((16,)),
            dma((16,)), dma((16,)), dma((16,)), dma((16,)),
        ],
        compiler_params=pltpu.CompilerParams(
            collective_id=0, has_side_effects=True, vmem_limit_bytes=48 * 1024 * 1024
        ),
        name="handoff",
    )(
        resident_kv, resident_query, resident_new, lengths, fresh_kv,
        handed_query.reshape(16, 8, 2, 1024), fresh_new, matching,
    )
    return (
        ro,
        ho.reshape(1, 16, 8, 2, 1024),
        hc.reshape(1, 1, 8, 2, 16, 2048),
    )


def solution(mesh):
    return jax.shard_map(
        body,
        mesh=mesh,
        in_specs=(
            P(("side", "grp", "tp"), None, None),
            P(("side", "grp"), "tp"),
            P(("side", "grp", "tp"), None),
            P(("side", "grp", "tp")),
            P(("side", "grp", "tp"), None, None),
            P(("side", "grp"), None, None, None, "tp"),
            P(("side", "grp", "tp"), None),
            P(("side", "grp", "tp"), None),
        ),
        out_specs=(
            P(("side", "grp"), "tp"),
            P(("side", "grp"), None, None, None, "tp"),
            P(("side", "grp"), "tp", None, None, None, None),
        ),
        check_vma=False,
    )
```

```python
import math

import jax
import jax.numpy as jnp
from jax import lax
from jax.experimental import pallas as pl
from jax.experimental.pallas import tpu as pltpu
from jax.sharding import PartitionSpec as P

MESH = pl.DeviceIdType.MESH
BF = jnp.bfloat16
F32 = jnp.float32
HD = 128
KVH = 8
N_GRP = 8
N_TP = 16
NEG_FILL = -1e30
SCALE = 1.0 / math.sqrt(HD)
LAG = 2
FIRST = "kkqkqkqkqkkk"
LAST = "kkkkkqkqkqkq"


def iota(shape, dim):
    return lax.broadcasted_iota(jnp.int32, shape, dim)


def attend(q, k, v, new_k, new_v, valid):
    s = lax.dot_general(q, k, (((1,), (1,)), ((), ())), preferred_element_type=F32) * SCALE
    s = jnp.where(valid, s, NEG_FILL)
    sn = jnp.sum(q.astype(F32) * new_k, axis=-1, keepdims=True) * SCALE
    top = jnp.maximum(jnp.max(s, axis=-1, keepdims=True), sn)
    p = jnp.exp(s - top)
    pn = jnp.exp(sn - top)
    total = jnp.sum(p, axis=-1, keepdims=True) + pn
    numer = jnp.dot(p.astype(BF), v, preferred_element_type=F32)
    numer = numer + pn.astype(BF).astype(F32) * new_v
    return (numer / total).astype(BF)


def kernel(
    kv_any, rq_any, rn_any, len_any, fkv_any, hq_any, fn_any, mt_any,
    ro_ref, ho_ref, kvb,
    rq_v, rn_v, len_s, fn_v, mt_v,
    rkv, rqf, rqt, rqs, rqb, ros, rob, rof, rot, place_s, place_r, new_s, new_r,
    npk, nb, land, sel, pk, qb, osd,
    loc, pls, plr, nws, nwr, s1s, s1r, nys, nyr, s2s, s2r, rqss, rqr, qs, qr, rosm, ror, os_, orr,
):
    side = lax.axis_index("side")
    g = lax.axis_index("grp")
    i = lax.axis_index("tp")
    sp = (side + 2) % 4
    x, zh = i // 4, i % 4

    def head(p):
        return 2 * ((x + p) % 4) + p // 4

    def remote(src, dst, ss, rs, **dev):
        return pltpu.make_async_remote_copy(
            src_ref=src, dst_ref=dst, send_sem=ss, recv_sem=rs, device_id=dev, device_id_type=MESH
        )

    def span(low, high, f):
        def body(k, _):
            f(k)
            return 0

        lax.fori_loop(low, high, body, 0)

    def over(n, f):
        def body(k, _):
            f(k)
            return 0

        lax.fori_loop(0, n, body, 0)

    def d_stage1(h, part):
        cols = pl.ds(pl.multiple_of(part * KVH * HD + h * HD, 128), HD)
        return remote(
            fkv_any.at[:, :, cols], land.at[h, :, :, pl.ds(part * HD, HD)],
            s1s.at[h, part], s1r.at[h, part], side=sp,
        )

    def d_place():
        return remote(place_s, place_r, pls, plr, side=sp)

    def d_new():
        return remote(new_s, new_r, nws, nwr, side=sp)

    def d_new_y(d, me):
        return remote(npk.at[d], nb.at[me], nys.at[d], nyr.at[me], grp=d)

    def d_kv_y(c, d, me):
        return remote(pk.at[c, d], kvb.at[c, me], s2s.at[c, d], s2r.at[c, me], grp=d)

    def d_rq(t, me):
        return remote(rqs.at[t], rqb.at[me], rqss.at[t], rqr.at[me], tp=t)

    def d_q(t, me):
        return remote(hq_any.at[t], qb.at[me], qs.at[t], qr.at[me], tp=t)

    def d_ro(t, me):
        return remote(ros.at[t], rob.at[me], rosm.at[t], ror.at[me], tp=t)

    def d_out(t, me):
        return remote(osd.at[t], ho_ref.at[me], os_.at[t], orr.at[me], tp=t)

    def local(src, dst, at):
        return pltpu.make_async_copy(src, dst, loc.at[at])

    def l_kv():
        return local(kv_any, rkv, 0)

    def l_q():
        return local(hq_any.at[i], qb.at[i], 1)

    def l_out():
        return local(osd.at[i], ho_ref.at[i], 2)

    small = [
        local(mt_any, mt_v, 3), local(rq_any, rq_v, 4), local(fn_any, fn_v, 5),
        local(rn_any, rn_v, 6), local(len_any, len_s, 7),
    ]

    def tp_peer(k):
        return (i + N_TP - 1 - k) % N_TP

    def grp_peer(k):
        return (g + 1 + k) % N_GRP

    barrier = pltpu.get_barrier_semaphore()
    over(N_TP - 1, lambda k: pl.semaphore_signal(
        barrier, inc=1, device_id={"tp": tp_peer(k)}, device_id_type=MESH))
    over(N_GRP - 1, lambda k: pl.semaphore_signal(
        barrier, inc=1, device_id={"grp": grp_peer(k)}, device_id_type=MESH))
    pl.semaphore_signal(barrier, inc=1, device_id={"side": sp}, device_id_type=MESH)
    for copy in small:
        copy.start()
    l_q().start()
    l_kv().start()
    for copy in small:
        copy.wait()

    row, lane = iota((8, 128), 0), iota((8, 128), 1)
    across = jnp.broadcast_to(mt_v[...], (8, 8))
    down = jnp.sum(jnp.where(iota((8, 8), 0) == iota((8, 8), 1), across, 0), axis=1, keepdims=True)
    m = jnp.broadcast_to(down, (8, 128))

    def places(req):
        mrow = jnp.sum(jnp.where(row == req, m, 0), axis=0, keepdims=True)
        mine = jnp.broadcast_to(mrow, (8, 128))
        rank = jnp.sum(jnp.where((m == mine) & (row < req), 1, 0), axis=0, keepdims=True)
        return jnp.broadcast_to(mrow * 2 + rank, (8, 128))

    wide = places(lane // 16) * 16 + lane % 16
    narrow = jnp.where(lane < 8, places(lane), -1)
    place_s[...] = jnp.where(row < 4, wide, narrow)
    new_s[...] = jnp.concatenate([fn_v[...], jnp.zeros((8, 2 * KVH * HD), BF)], axis=0)
    for j in range(8):
        rqf[32 * j:32 * j + 32] = rq_v[:, 128 * j:128 * j + 128].astype(F32)
    for j in range(8):
        for r in range(2):
            rqt[pl.ds(2 * j + r, 16, stride=16), :] = rqf[pl.ds(32 * j + r, 16, stride=2), :]
    rqs[...] = rqt[...].astype(BF).reshape(16, 16, 128)
    rqb[i] = rqs[i]

    pl.semaphore_wait(barrier, N_TP + N_GRP - 1)

    def send_all(turns):
        k = q = 0
        for turn in turns:
            if turn == "k":
                d_stage1(head(k), 0).start()
                d_stage1(head(k), 1).start()
                k += 1
            else:
                for dz in range(4):
                    if q or dz:
                        d_q((x + 4 - q) % 4 * 4 + (zh + dz) % 4, i).start()
                q += 1
            if k == 1 and q == 0:
                over(N_TP - 1, lambda n: d_rq(tp_peer(n), i).start())

    d_place().start()
    d_new().start()

    @pl.when(zh < 2)
    def _():
        send_all(FIRST)

    @pl.when(zh >= 2)
    def _():
        send_all(LAST)

    d_place().wait_recv()
    sel[...] = jnp.where(iota((256, 128), 0) == place_r[0:1, :], 1.0, 0.0).astype(BF)
    sel16 = jnp.where(iota((16, 16), 0) == place_r[4:5, 0:16], 1.0, 0.0).astype(BF)

    def pack(p):
        h = head(p)
        d_stage1(h, 0).wait_recv()
        d_stage1(h, 1).wait_recv()
        x = land[h].reshape(128, 2 * HD)
        y = jnp.dot(sel[...], x, preferred_element_type=F32).astype(BF)
        pk[h] = y.reshape(8, 32, 2 * HD)
        over(N_GRP - 1, lambda k: d_kv_y(h, grp_peer(k), g).start())
        kvb[h, g] = pk[h, g]

    def pack_new():
        d_new().wait_recv()
        for c in range(16):
            cols = slice(128 * c, 128 * c + 128)
            y = jnp.dot(sel16, new_r[:, cols], preferred_element_type=F32).astype(BF)
            npk[:, :, cols] = y.reshape(8, 2, 128)
        over(N_GRP - 1, lambda k: d_new_y(grp_peer(k), g).start())
        nb[g] = npk[g]

    rrow, rcol = iota((32, 512), 0) % 2, iota((32, 512), 1)
    length = jnp.where(rrow == 0, len_s[0], len_s[1])
    rvalid = (rcol // 256 == rrow) & (rcol % 256 < length)
    first = iota((32, 128), 0) % 2 == 0

    def resident(h):
        q = jnp.concatenate([rqb[2 * h], rqb[2 * h + 1]], axis=0)
        kcols = pl.ds(pl.multiple_of(h * 128, 128), 128)
        vcols = pl.ds(pl.multiple_of(KVH * HD + h * 128, 128), 128)
        k = rkv[:, :, kcols].reshape(512, 128)
        v = rkv[:, :, vcols].reshape(512, 128)
        nk = rn_v[:, kcols].astype(F32)
        nv = rn_v[:, vcols].astype(F32)
        o = attend(
            q, k, v, jnp.where(first, nk[0:1], nk[1:2]), jnp.where(first, nv[0:1], nv[1:2]), rvalid
        )
        ros[2 * h] = o[0:16]
        ros[2 * h + 1] = o[16:32]

    def resident_all():
        l_kv().wait()
        over(N_TP - 1, lambda k: d_rq(tp_peer(k), tp_peer(k)).wait_recv())
        over(KVH, resident)
        over(N_TP - 1, lambda k: d_ro(tp_peer(k), i).start())
        rob[i] = ros[i]

    hvalid = iota((256, 256), 0) % 16 == iota((256, 256), 1) // 16

    def handed(p):
        h = head(p)
        over(N_GRP - 1, lambda k: d_kv_y(h, grp_peer(k), grp_peer(k)).wait_recv())
        for t2 in range(2):
            @pl.when(2 * h + t2 != i)
            def _():
                d_q(2 * h + t2, 2 * h + t2).wait_recv()
        q = jnp.concatenate(
            [
                qb[2 * h + t2, :, :, 128 * j:128 * j + 128].reshape(16, 128)
                for t2 in range(2) for j in range(8)
            ],
            axis=0,
        )
        k = kvb[h, :, :, 0:128].reshape(256, 128)
        v = kvb[h, :, :, 128:256].reshape(256, 128)
        kcols = pl.ds(pl.multiple_of(h * 128, 128), 128)
        vcols = pl.ds(pl.multiple_of(KVH * HD + h * 128, 128), 128)
        nk = nb[:, :, kcols].reshape(16, 128).astype(F32)
        nv = nb[:, :, vcols].reshape(16, 128).astype(F32)
        o = attend(q, k, v, jnp.tile(nk, (16, 1)), jnp.tile(nv, (16, 1)), hvalid)
        for t2 in range(2):
            for j in range(8):
                at = 16 * (8 * t2 + j)
                osd[2 * h + t2, :, :, 128 * j:128 * j + 128] = o[at:at + 16].reshape(8, 2, 128)
        for t2 in range(2):
            @pl.when(2 * h + t2 != i)
            def _():
                d_out(2 * h + t2, i).start()

    span(0, LAG, pack)
    pack_new()
    resident_all()
    over(N_GRP - 1, lambda k: d_new_y(grp_peer(k), grp_peer(k)).wait_recv())
    l_q().wait()

    def both(p):
        pack(p)
        handed(p - LAG)

    span(LAG, KVH, both)
    span(KVH - LAG, KVH, handed)
    l_out().start()

    over(N_TP - 1, lambda k: d_ro(tp_peer(k), tp_peer(k)).wait_recv())
    rof[...] = rob[...].reshape(256, 128).astype(F32)
    for j in range(8):
        for r in range(2):
            rot[pl.ds(32 * j + r, 16, stride=2), :] = rof[pl.ds(2 * j + r, 16, stride=16), :]
    for j in range(8):
        ro_ref[:, 128 * j:128 * j + 128] = rot[32 * j:32 * j + 32].astype(BF)

    d_place().wait_send()
    d_new().wait_send()

    def end_chunk(c):
        for part in range(2):
            d_stage1(c, part).wait_send()
        over(N_GRP - 1, lambda k: d_kv_y(c, grp_peer(k), g).wait_send())

    over(KVH, end_chunk)
    over(N_GRP - 1, lambda k: d_new_y(grp_peer(k), g).wait_send())

    def end_tp(k):
        t = tp_peer(k)
        d_rq(t, i).wait_send()
        d_q(t, i).wait_send()
        d_ro(t, i).wait_send()
        d_out(t, i).wait_send()
        d_out(t, t).wait_recv()

    over(N_TP - 1, end_tp)
    l_out().wait()


def write_kernel(ro, ho, kvb, ro_o, ho_o, hc_o, sems):
    copies = [
        pltpu.make_async_copy(ro, ro_o, sems.at[0]),
        pltpu.make_async_copy(ho, ho_o, sems.at[1]),
    ]
    for h in range(KVH):
        for part in range(2):
            copies.append(pltpu.make_async_copy(
                kvb.at[h, :, :, pl.ds(part * HD, HD)],
                hc_o.at[:, :, pl.ds((part * KVH + h) * HD, HD)],
                sems.at[2 + 2 * h + part],
            ))
    for copy in copies:
        copy.start()
    for copy in copies:
        copy.wait()


def body(
    resident_kv, resident_query, resident_new, lengths, fresh_kv, handed_query, fresh_new, matching
):
    vm = pl.BlockSpec(memory_space=pltpu.VMEM)
    hbm = pl.BlockSpec(memory_space=pltpu.HBM)
    dma = pltpu.SemaphoreType.DMA
    results = (
        jax.ShapeDtypeStruct((32, 1024), BF),
        jax.ShapeDtypeStruct((16, 8, 2, 1024), BF),
    )
    ro, ho, kvb = pl.pallas_call(
        kernel,
        out_shape=results + (jax.ShapeDtypeStruct((KVH, 8, 32, 2 * HD), BF),),
        in_specs=[hbm] * 8,
        out_specs=(vm, vm, vm),
        scratch_shapes=[
            pltpu.VMEM((32, 1024), BF),
            pltpu.VMEM((2, 2048), BF),
            pltpu.SMEM((2,), jnp.int32),
            pltpu.VMEM((8, 2048), BF),
            pltpu.VMEM((1, 8), jnp.int32),
            pltpu.VMEM((2, 256, 2048), BF),
            pltpu.VMEM((256, 128), F32),
            pltpu.VMEM((256, 128), F32),
            pltpu.VMEM((16, 16, 128), BF),
            pltpu.VMEM((16, 16, 128), BF),
            pltpu.VMEM((16, 16, 128), BF),
            pltpu.VMEM((16, 16, 128), BF),
            pltpu.VMEM((256, 128), F32),
            pltpu.VMEM((256, 128), F32),
            pltpu.VMEM((8, 128), jnp.int32),
            pltpu.VMEM((8, 128), jnp.int32),
            pltpu.VMEM((16, 2048), BF),
            pltpu.VMEM((16, 2048), BF),
            pltpu.VMEM((8, 2, 2048), BF),
            pltpu.VMEM((8, 2, 2048), BF),
            pltpu.VMEM((KVH, 8, 16, 2 * HD), BF),
            pltpu.VMEM((256, 128), BF),
            pltpu.VMEM((KVH, 8, 32, 2 * HD), BF),
            pltpu.VMEM((16, 8, 2, 1024), BF),
            pltpu.VMEM((16, 8, 2, 1024), BF),
            dma((8,)),
            dma, dma, dma, dma,
            dma((KVH, 2)), dma((KVH, 2)),
            dma((8,)), dma((8,)),
            dma((KVH, 8)), dma((KVH, 8)),
            dma((16,)), dma((16,)), dma((16,)), dma((16,)),
            dma((16,)), dma((16,)), dma((16,)), dma((16,)),
        ],
        compiler_params=pltpu.CompilerParams(
            collective_id=0, has_side_effects=True, vmem_limit_bytes=40 * 1024 * 1024
        ),
        name="handoff",
    )(*(
        pltpu.with_memory_space_constraint(array, pltpu.HBM)
        for array in (
            resident_kv, resident_query, resident_new, lengths, fresh_kv,
            handed_query.reshape(16, 8, 2, 1024), fresh_new, matching.reshape(1, 8),
        )
    ))
    ro, ho, hc = pl.pallas_call(
        write_kernel,
        out_shape=results + (jax.ShapeDtypeStruct((8, 32, 2048), BF),),
        in_specs=[vm] * 3,
        out_specs=(hbm, hbm, hbm),
        scratch_shapes=[dma((2 + 2 * KVH,))],
        compiler_params=pltpu.CompilerParams(vmem_limit_bytes=4 * 1024 * 1024),
        name="write",
    )(*(pltpu.with_memory_space_constraint(array, pltpu.VMEM) for array in (ro, ho, kvb)))
    return (
        ro,
        ho.reshape(1, 16, 8, 2, 1024),
        hc.reshape(1, 1, 8, 2, 16, 2048),
    )


def solution(mesh):
    return jax.shard_map(
        body,
        mesh=mesh,
        in_specs=(
            P(("side", "grp", "tp"), None, None),
            P(("side", "grp"), "tp"),
            P(("side", "grp", "tp"), None),
            P(("side", "grp", "tp")),
            P(("side", "grp", "tp"), None, None),
            P(("side", "grp"), None, None, None, "tp"),
            P(("side", "grp", "tp"), None),
            P(("side", "grp", "tp"), None),
        ),
        out_specs=(
            P(("side", "grp"), "tp"),
            P(("side", "grp"), None, None, None, "tp"),
            P(("side", "grp"), "tp", None, None, None, None),
        ),
        check_vma=False,
    )
```

```python
import math

import jax
import jax.numpy as jnp
from jax import lax
from jax.experimental import pallas as pl
from jax.experimental.pallas import tpu as pltpu
from jax.sharding import PartitionSpec as P

MESH = pl.DeviceIdType.MESH
BF = jnp.bfloat16
F32 = jnp.float32
HD = 128
KVH = 8
N_GRP = 8
N_TP = 16
NEG_FILL = -1e30
SCALE = 1.0 / math.sqrt(HD)
LAG = 3
AHEAD = 4
RESIDENT_AT = 5
Q_FROM = 0


def iota(shape, dim):
    return lax.broadcasted_iota(jnp.int32, shape, dim)


def attend(q, k, v, new_k, new_v, valid):
    s = lax.dot_general(q, k, (((1,), (1,)), ((), ())), preferred_element_type=F32) * SCALE
    s = jnp.where(valid, s, NEG_FILL)
    sn = jnp.sum(q.astype(F32) * new_k, axis=-1, keepdims=True) * SCALE
    top = jnp.maximum(jnp.max(s, axis=-1, keepdims=True), sn)
    p = jnp.exp(s - top)
    pn = jnp.exp(sn - top)
    total = jnp.sum(p, axis=-1, keepdims=True) + pn
    numer = jnp.dot(p.astype(BF), v, preferred_element_type=F32)
    numer = numer + pn.astype(BF).astype(F32) * new_v
    return (numer / total).astype(BF)


def kernel(
    kv_any, rq_any, rn_any, len_any, fkv_any, hq_any, fn_any, mt_any,
    ro_ref, ho_ref, kvb,
    rq_v, rn_v, len_s, fn_v, mt_v,
    rkv, rqf, rqt, rqs, rqb, ros, rob, rof, rot, place_s, place_r, new_s, new_r,
    npk, nb, land, sel, pk, qb, osd,
    loc, pls, plr, nws, nwr, s1s, s1r, nys, nyr, s2s, s2r, rqss, rqr, qs, qr, rosm, ror, os_, orr,
):
    side = lax.axis_index("side")
    g = lax.axis_index("grp")
    i = lax.axis_index("tp")
    sp = (side + 2) % 4
    x, zh = i // 4, i % 4

    def head(p):
        return 2 * ((x + p) % 4) + p // 4

    def remote(src, dst, ss, rs, **dev):
        return pltpu.make_async_remote_copy(
            src_ref=src, dst_ref=dst, send_sem=ss, recv_sem=rs, device_id=dev, device_id_type=MESH
        )

    def span(low, high, f):
        def body(k, _):
            f(k)
            return 0

        lax.fori_loop(low, high, body, 0)

    def over(n, f):
        def body(k, _):
            f(k)
            return 0

        lax.fori_loop(0, n, body, 0)

    def d_stage1(h, part):
        cols = pl.ds(pl.multiple_of(part * KVH * HD + h * HD, 128), HD)
        return remote(
            fkv_any.at[:, :, cols], land.at[h, :, :, pl.ds(part * HD, HD)],
            s1s.at[h, part], s1r.at[h, part], side=sp,
        )

    def d_place():
        return remote(place_s, place_r, pls, plr, side=sp)

    def d_new():
        return remote(new_s, new_r, nws, nwr, side=sp)

    def d_new_y(d, me):
        return remote(npk.at[d], nb.at[me], nys, nyr, grp=d)

    def d_kv_y(c, d, me):
        return remote(pk.at[c, d], kvb.at[c, me], s2s, s2r.at[c], grp=d)

    def d_rq(t, me):
        return remote(rqs.at[t], rqb.at[me], rqss, rqr, tp=t)

    def d_q(t, me):
        return remote(hq_any.at[t], qb.at[me], qs, qr.at[me], tp=t)

    def d_ro(t, me):
        return remote(ros.at[t], rob.at[me], rosm, ror, tp=t)

    def d_out(t, me):
        return remote(osd.at[t], ho_ref.at[me], os_, orr, tp=t)

    def all_new_y():
        return remote(npk.at[pl.ds(0, 7)], nb.at[pl.ds(0, 7)], nys, nyr, grp=g)

    def all_kv_y(c):
        return remote(pk.at[c, pl.ds(0, 7)], kvb.at[c, pl.ds(0, 7)], s2s, s2r.at[c], grp=g)

    def all_kv_sent():
        return remote(pk.at[pl.ds(0, 7)], kvb.at[pl.ds(0, 7)], s2s, s2r.at[0], grp=g)

    def all_tp(src, dst, ss, rs):
        return remote(src.at[pl.ds(0, 15)], dst.at[pl.ds(0, 15)], ss, rs, tp=i)

    def local(src, dst, at):
        return pltpu.make_async_copy(src, dst, loc.at[at])

    def l_kv():
        return local(kv_any, rkv, 0)

    def l_q():
        return local(hq_any.at[i], qb.at[i], 1)

    def l_out():
        return local(osd.at[i], ho_ref.at[i], 2)

    small = [
        local(mt_any, mt_v, 3), local(rq_any, rq_v, 4), local(fn_any, fn_v, 5),
        local(rn_any, rn_v, 6), local(len_any, len_s, 7),
    ]

    def tp_peer(k):
        return (i + N_TP - 1 - k) % N_TP

    def grp_peer(k):
        return (g + 1 + k) % N_GRP

    barrier = pltpu.get_barrier_semaphore()
    over(N_TP - 1, lambda k: pl.semaphore_signal(
        barrier, inc=1, device_id={"tp": tp_peer(k)}, device_id_type=MESH))
    over(N_GRP - 1, lambda k: pl.semaphore_signal(
        barrier, inc=1, device_id={"grp": grp_peer(k)}, device_id_type=MESH))
    pl.semaphore_signal(barrier, inc=1, device_id={"side": sp}, device_id_type=MESH)
    for copy in small:
        copy.start()
    l_q().start()
    l_kv().start()
    def start1(p):
        d_stage1(head(p), 0).start()
        d_stage1(head(p), 1).start()

    def start_q(n):
        def one(dz):
            t = (x + 4 - n) % 4 * 4 + (zh + dz) % 4

            @pl.when(t != i)
            def _():
                d_q(t, i).start()

        over(4, one)

    pl.semaphore_wait(barrier, N_TP + N_GRP - 1)

    span(0, AHEAD, start1)
    for copy in small:
        copy.wait()

    row, lane = iota((8, 128), 0), iota((8, 128), 1)
    across = jnp.broadcast_to(mt_v[...], (8, 8))
    down = jnp.sum(jnp.where(iota((8, 8), 0) == iota((8, 8), 1), across, 0), axis=1, keepdims=True)
    m = jnp.broadcast_to(down, (8, 128))

    def places(req):
        mrow = jnp.sum(jnp.where(row == req, m, 0), axis=0, keepdims=True)
        mine = jnp.broadcast_to(mrow, (8, 128))
        rank = jnp.sum(jnp.where((m == mine) & (row < req), 1, 0), axis=0, keepdims=True)
        return jnp.broadcast_to(mrow * 2 + rank, (8, 128))

    wide = places(lane // 16) * 16 + lane % 16
    narrow = jnp.where(lane < 8, places(lane), -1)
    place_s[...] = jnp.where(row < 4, wide, narrow)
    new_s[...] = jnp.concatenate([fn_v[...], jnp.zeros((8, 2 * KVH * HD), BF)], axis=0)
    for j in range(8):
        rqf[32 * j:32 * j + 32] = rq_v[:, 128 * j:128 * j + 128].astype(F32)
    for j in range(8):
        for r in range(2):
            rqt[pl.ds(2 * j + r, 16, stride=16), :] = rqf[pl.ds(32 * j + r, 16, stride=2), :]
    rqs[...] = rqt[...].astype(BF).reshape(16, 16, 128)
    rqb[i] = rqs[i]

    d_place().start()
    d_new().start()
    over(N_TP - 1, lambda n: d_rq(tp_peer(n), i).start())
    d_place().wait_recv()
    sel[...] = jnp.where(iota((256, 128), 0) == place_r[0:1, :], 1.0, 0.0).astype(BF)
    sel16 = jnp.where(iota((16, 16), 0) == place_r[4:5, 0:16], 1.0, 0.0).astype(BF)

    def pack(p):
        h = head(p)
        d_stage1(h, 0).wait_recv()
        d_stage1(h, 1).wait_recv()
        x = land[h].reshape(128, 2 * HD)
        y = jnp.dot(sel[...], x, preferred_element_type=F32).astype(BF)
        pk[h] = y.reshape(8, 32, 2 * HD)
        over(N_GRP - 1, lambda k: d_kv_y(h, grp_peer(k), g).start())
        kvb[h, g] = pk[h, g]

        @pl.when(p + AHEAD < KVH)
        def _():
            start1(p + AHEAD)

        @pl.when((p >= Q_FROM) & (p < Q_FROM + 4))
        def _():
            start_q(p - Q_FROM)

    def pack_new():
        d_new().wait_recv()
        for c in range(16):
            cols = slice(128 * c, 128 * c + 128)
            y = jnp.dot(sel16, new_r[:, cols], preferred_element_type=F32).astype(BF)
            npk[:, :, cols] = y.reshape(8, 2, 128)
        over(N_GRP - 1, lambda k: d_new_y(grp_peer(k), g).start())
        nb[g] = npk[g]

    rrow, rcol = iota((32, 512), 0) % 2, iota((32, 512), 1)
    length = jnp.where(rrow == 0, len_s[0], len_s[1])
    rvalid = (rcol // 256 == rrow) & (rcol % 256 < length)
    first = iota((32, 128), 0) % 2 == 0

    def resident(h):
        q = jnp.concatenate([rqb[2 * h], rqb[2 * h + 1]], axis=0)
        kcols = pl.ds(pl.multiple_of(h * 128, 128), 128)
        vcols = pl.ds(pl.multiple_of(KVH * HD + h * 128, 128), 128)
        k = rkv[:, :, kcols].reshape(512, 128)
        v = rkv[:, :, vcols].reshape(512, 128)
        nk = rn_v[:, kcols].astype(F32)
        nv = rn_v[:, vcols].astype(F32)
        o = attend(
            q, k, v, jnp.where(first, nk[0:1], nk[1:2]), jnp.where(first, nv[0:1], nv[1:2]), rvalid
        )
        ros[2 * h] = o[0:16]
        ros[2 * h + 1] = o[16:32]

    def resident_all():
        l_kv().wait()
        all_tp(rqs, rqb, rqss, rqr).wait_recv()
        over(KVH, resident)
        over(N_TP - 1, lambda k: d_ro(tp_peer(k), i).start())
        rob[i] = ros[i]

    hvalid = iota((256, 256), 0) % 16 == iota((256, 256), 1) // 16

    def handed(p):
        h = head(p)
        all_kv_y(h).wait_recv()
        for t2 in range(2):
            @pl.when(2 * h + t2 != i)
            def _():
                d_q(2 * h + t2, 2 * h + t2).wait_recv()
        q = jnp.concatenate(
            [
                qb[2 * h + t2, :, :, 128 * j:128 * j + 128].reshape(16, 128)
                for t2 in range(2) for j in range(8)
            ],
            axis=0,
        )
        k = kvb[h, :, :, 0:128].reshape(256, 128)
        v = kvb[h, :, :, 128:256].reshape(256, 128)
        kcols = pl.ds(pl.multiple_of(h * 128, 128), 128)
        vcols = pl.ds(pl.multiple_of(KVH * HD + h * 128, 128), 128)
        nk = nb[:, :, kcols].reshape(16, 128).astype(F32)
        nv = nb[:, :, vcols].reshape(16, 128).astype(F32)
        o = attend(q, k, v, jnp.tile(nk, (16, 1)), jnp.tile(nv, (16, 1)), hvalid)
        for t2 in range(2):
            for j in range(8):
                at = 16 * (8 * t2 + j)
                osd[2 * h + t2, :, :, 128 * j:128 * j + 128] = o[at:at + 16].reshape(8, 2, 128)
        for t2 in range(2):
            @pl.when(2 * h + t2 != i)
            def _():
                d_out(2 * h + t2, i).start()

    span(0, LAG, pack)
    pack_new()
    all_new_y().wait_recv()
    l_q().wait()

    def both(p):
        pack(p)
        handed(p - LAG)

    span(LAG, RESIDENT_AT, both)
    resident_all()
    span(RESIDENT_AT, KVH, both)
    span(KVH - LAG, KVH, handed)
    l_out().start()

    all_tp(ros, rob, rosm, ror).wait_recv()
    rof[...] = rob[...].reshape(256, 128).astype(F32)
    for j in range(8):
        for r in range(2):
            rot[pl.ds(32 * j + r, 16, stride=2), :] = rof[pl.ds(2 * j + r, 16, stride=16), :]
    for j in range(8):
        ro_ref[:, 128 * j:128 * j + 128] = rot[32 * j:32 * j + 32].astype(BF)

    d_place().wait_send()
    d_new().wait_send()

    def end_kv(h):
        d_stage1(h, 0).wait_send()
        d_stage1(h, 1).wait_send()

    over(KVH, end_kv)
    all_kv_sent().wait_send()
    all_new_y().wait_send()
    all_tp(rqs, rqb, rqss, rqr).wait_send()
    all_tp(hq_any, qb, qs, qr.at[i]).wait_send()
    all_tp(ros, rob, rosm, ror).wait_send()
    all_tp(osd, ho_ref, os_, orr).wait_send()
    all_tp(osd, ho_ref, os_, orr).wait_recv()
    l_out().wait()


def write_kernel(ro, ho, kvb, ro_o, ho_o, hc_o, sems):
    copies = [
        pltpu.make_async_copy(ro, ro_o, sems.at[0]),
        pltpu.make_async_copy(ho, ho_o, sems.at[1]),
    ]
    for h in range(KVH):
        for part in range(2):
            copies.append(pltpu.make_async_copy(
                kvb.at[h, :, :, pl.ds(part * HD, HD)],
                hc_o.at[:, :, pl.ds((part * KVH + h) * HD, HD)],
                sems.at[2 + 2 * h + part],
            ))
    for copy in copies:
        copy.start()
    for copy in copies:
        copy.wait()


def body(
    resident_kv, resident_query, resident_new, lengths, fresh_kv, handed_query, fresh_new, matching
):
    vm = pl.BlockSpec(memory_space=pltpu.VMEM)
    hbm = pl.BlockSpec(memory_space=pltpu.HBM)
    dma = pltpu.SemaphoreType.DMA
    results = (
        jax.ShapeDtypeStruct((32, 1024), BF),
        jax.ShapeDtypeStruct((16, 8, 2, 1024), BF),
    )
    ro, ho, kvb = pl.pallas_call(
        kernel,
        out_shape=results + (jax.ShapeDtypeStruct((KVH, 8, 32, 2 * HD), BF),),
        in_specs=[hbm] * 8,
        out_specs=(vm, vm, vm),
        scratch_shapes=[
            pltpu.VMEM((32, 1024), BF),
            pltpu.VMEM((2, 2048), BF),
            pltpu.SMEM((2,), jnp.int32),
            pltpu.VMEM((8, 2048), BF),
            pltpu.VMEM((1, 8), jnp.int32),
            pltpu.VMEM((2, 256, 2048), BF),
            pltpu.VMEM((256, 128), F32),
            pltpu.VMEM((256, 128), F32),
            pltpu.VMEM((16, 16, 128), BF),
            pltpu.VMEM((16, 16, 128), BF),
            pltpu.VMEM((16, 16, 128), BF),
            pltpu.VMEM((16, 16, 128), BF),
            pltpu.VMEM((256, 128), F32),
            pltpu.VMEM((256, 128), F32),
            pltpu.VMEM((8, 128), jnp.int32),
            pltpu.VMEM((8, 128), jnp.int32),
            pltpu.VMEM((16, 2048), BF),
            pltpu.VMEM((16, 2048), BF),
            pltpu.VMEM((8, 2, 2048), BF),
            pltpu.VMEM((8, 2, 2048), BF),
            pltpu.VMEM((KVH, 8, 16, 2 * HD), BF),
            pltpu.VMEM((256, 128), BF),
            pltpu.VMEM((KVH, 8, 32, 2 * HD), BF),
            pltpu.VMEM((16, 8, 2, 1024), BF),
            pltpu.VMEM((16, 8, 2, 1024), BF),
            dma((8,)),
            dma, dma, dma, dma,
            dma((KVH, 2)), dma((KVH, 2)),
            dma, dma,
            dma, dma((KVH,)),
            dma, dma, dma, dma((16,)),
            dma, dma, dma, dma,
        ],
        compiler_params=pltpu.CompilerParams(
            collective_id=0, has_side_effects=True, vmem_limit_bytes=40 * 1024 * 1024
        ),
        name="handoff",
    )(*(
        pltpu.with_memory_space_constraint(array, pltpu.HBM)
        for array in (
            resident_kv, resident_query, resident_new, lengths, fresh_kv,
            handed_query.reshape(16, 8, 2, 1024), fresh_new, matching.reshape(1, 8),
        )
    ))
    ro, ho, hc = pl.pallas_call(
        write_kernel,
        out_shape=results + (jax.ShapeDtypeStruct((8, 32, 2048), BF),),
        in_specs=[vm] * 3,
        out_specs=(hbm, hbm, hbm),
        scratch_shapes=[dma((2 + 2 * KVH,))],
        compiler_params=pltpu.CompilerParams(vmem_limit_bytes=4 * 1024 * 1024),
        name="write",
    )(*(pltpu.with_memory_space_constraint(array, pltpu.VMEM) for array in (ro, ho, kvb)))
    return (
        ro,
        ho.reshape(1, 16, 8, 2, 1024),
        hc.reshape(1, 1, 8, 2, 16, 2048),
    )


def solution(mesh):
    return jax.shard_map(
        body,
        mesh=mesh,
        in_specs=(
            P(("side", "grp", "tp"), None, None),
            P(("side", "grp"), "tp"),
            P(("side", "grp", "tp"), None),
            P(("side", "grp", "tp")),
            P(("side", "grp", "tp"), None, None),
            P(("side", "grp"), None, None, None, "tp"),
            P(("side", "grp", "tp"), None),
            P(("side", "grp", "tp"), None),
        ),
        out_specs=(
            P(("side", "grp"), "tp"),
            P(("side", "grp"), None, None, None, "tp"),
            P(("side", "grp"), "tp", None, None, None, None),
        ),
        check_vma=False,
    )
```

```python
import math

import jax
import jax.numpy as jnp
from jax import lax
from jax.experimental import pallas as pl
from jax.experimental.pallas import tpu as pltpu
from jax.sharding import PartitionSpec as P

MESH = pl.DeviceIdType.MESH
BF = jnp.bfloat16
F32 = jnp.float32
HD = 128
KVH = 8
N_GRP = 8
N_TP = 16
NEG_FILL = -1e30
SCALE = 1.0 / math.sqrt(HD)
LAG = 3
AHEAD = 4
RESIDENT_AT = 5
Q_FROM = 0


def iota(shape, dim):
    return lax.broadcasted_iota(jnp.int32, shape, dim)


def attend(q, k, v, new_k, new_v, valid):
    s = lax.dot_general(q, k, (((1,), (1,)), ((), ())), preferred_element_type=F32) * SCALE
    s = jnp.where(valid, s, NEG_FILL)
    sn = jnp.sum(q.astype(F32) * new_k, axis=-1, keepdims=True) * SCALE
    top = jnp.maximum(jnp.max(s, axis=-1, keepdims=True), sn)
    p = jnp.exp(s - top)
    pn = jnp.exp(sn - top)
    total = jnp.sum(p, axis=-1, keepdims=True) + pn
    numer = jnp.dot(p.astype(BF), v, preferred_element_type=F32)
    numer = numer + pn.astype(BF).astype(F32) * new_v
    return (numer / total).astype(BF)


def kernel(
    kv_any, rq_any, rn_any, len_any, fkv_any, hq_any, fn_any, mt_any,
    ro_ref, ho_ref, kvb,
    rq_v, rn_v, len_s, fn_v, mt_v,
    rkv, rqf, rqt, rqs, rqb, ros, rob, rof, rot, place_s, place_r, new_s, new_r,
    npk, nb, land, sel, pk, qb, osd,
    loc, pls, plr, nws, nwr, s1s, s1r, nys, nyr, s2s, s2r, rqss, rqr, qs, qr, rosm, ror, os_, orr,
):
    side = lax.axis_index("side")
    g = lax.axis_index("grp")
    i = lax.axis_index("tp")
    sp = (side + 2) % 4
    x, zh = i // 4, i % 4

    def head(p):
        alternate = side % 2
        step = p + alternate * (p // 2 - p)
        odd = p // 4 + alternate * (p % 2 - p // 4)
        return 2 * ((x + step) % 4) + odd

    def remote(src, dst, ss, rs, **dev):
        return pltpu.make_async_remote_copy(
            src_ref=src, dst_ref=dst, send_sem=ss, recv_sem=rs, device_id=dev, device_id_type=MESH
        )

    def span(low, high, f):
        def body(k, _):
            f(k)
            return 0

        lax.fori_loop(low, high, body, 0)

    def over(n, f):
        def body(k, _):
            f(k)
            return 0

        lax.fori_loop(0, n, body, 0)

    def d_stage1(h, part):
        cols = pl.ds(pl.multiple_of(part * KVH * HD + h * HD, 128), HD)
        return remote(
            fkv_any.at[:, :, cols], land.at[h, :, :, pl.ds(part * HD, HD)],
            s1s.at[h, part], s1r.at[h, part], side=sp,
        )

    def d_place():
        return remote(place_s, place_r, pls, plr, side=sp)

    def d_new():
        return remote(new_s, new_r, nws, nwr, side=sp)

    def d_new_y(d, me):
        return remote(npk.at[d], nb.at[me], nys, nyr, grp=d)

    def d_kv_y(c, d, me):
        return remote(pk.at[c, d], kvb.at[c, me], s2s, s2r.at[c], grp=d)

    def d_rq(t, me):
        return remote(rqs.at[t], rqb.at[me], rqss, rqr, tp=t)

    def d_q(t, me):
        return remote(hq_any.at[t], qb.at[me], qs, qr.at[me], tp=t)

    def d_ro(t, me):
        return remote(ros.at[t], rob.at[me], rosm, ror, tp=t)

    def d_out(t, me):
        return remote(osd.at[t], ho_ref.at[me], os_, orr, tp=t)

    def all_new_y():
        return remote(npk.at[pl.ds(0, 7)], nb.at[pl.ds(0, 7)], nys, nyr, grp=g)

    def all_kv_y(c):
        return remote(pk.at[c, pl.ds(0, 7)], kvb.at[c, pl.ds(0, 7)], s2s, s2r.at[c], grp=g)

    def all_kv_sent():
        return remote(pk.at[pl.ds(0, 7)], kvb.at[pl.ds(0, 7)], s2s, s2r.at[0], grp=g)

    def all_tp(src, dst, ss, rs):
        return remote(src.at[pl.ds(0, 15)], dst.at[pl.ds(0, 15)], ss, rs, tp=i)

    def local(src, dst, at):
        return pltpu.make_async_copy(src, dst, loc.at[at])

    def l_kv():
        return local(kv_any, rkv, 0)

    def l_q():
        return local(hq_any.at[i], qb.at[i], 1)

    def l_out():
        return local(osd.at[i], ho_ref.at[i], 2)

    small = [
        local(mt_any, mt_v, 3), local(rq_any, rq_v, 4), local(fn_any, fn_v, 5),
        local(rn_any, rn_v, 6), local(len_any, len_s, 7),
    ]

    def tp_peer(k):
        return (i + N_TP - 1 - k) % N_TP

    def grp_peer(k):
        return (g + 1 + k) % N_GRP

    barrier = pltpu.get_barrier_semaphore()
    over(N_TP - 1, lambda k: pl.semaphore_signal(
        barrier, inc=1, device_id={"tp": tp_peer(k)}, device_id_type=MESH))
    over(N_GRP - 1, lambda k: pl.semaphore_signal(
        barrier, inc=1, device_id={"grp": grp_peer(k)}, device_id_type=MESH))
    pl.semaphore_signal(barrier, inc=1, device_id={"side": sp}, device_id_type=MESH)
    for copy in small:
        copy.start()
    l_q().start()
    l_kv().start()
    def start1(p):
        d_stage1(head(p), 0).start()
        d_stage1(head(p), 1).start()

    def start_q(n):
        def one(dz):
            t = (x + 4 - n) % 4 * 4 + (zh + dz) % 4

            @pl.when(t != i)
            def _():
                d_q(t, i).start()

        over(4, one)

    pl.semaphore_wait(barrier, N_TP + N_GRP - 1)

    span(0, AHEAD, start1)
    for copy in small:
        copy.wait()

    row, lane = iota((8, 128), 0), iota((8, 128), 1)
    across = jnp.broadcast_to(mt_v[...], (8, 8))
    down = jnp.sum(jnp.where(iota((8, 8), 0) == iota((8, 8), 1), across, 0), axis=1, keepdims=True)
    m = jnp.broadcast_to(down, (8, 128))

    def places(req):
        mrow = jnp.sum(jnp.where(row == req, m, 0), axis=0, keepdims=True)
        mine = jnp.broadcast_to(mrow, (8, 128))
        rank = jnp.sum(jnp.where((m == mine) & (row < req), 1, 0), axis=0, keepdims=True)
        return jnp.broadcast_to(mrow * 2 + rank, (8, 128))

    wide = places(lane // 16) * 16 + lane % 16
    narrow = jnp.where(lane < 8, places(lane), -1)
    place_s[...] = jnp.where(row < 4, wide, narrow)
    new_s[...] = jnp.concatenate(
        [fn_v[:, 128 * c:128 * c + 128].astype(F32) for c in range(16)], axis=0
    ).astype(BF)
    for j in range(8):
        rqf[32 * j:32 * j + 32] = rq_v[:, 128 * j:128 * j + 128].astype(F32)
    for j in range(8):
        for r in range(2):
            rqt[pl.ds(2 * j + r, 16, stride=16), :] = rqf[pl.ds(32 * j + r, 16, stride=2), :]
    rqs[...] = rqt[...].astype(BF).reshape(16, 16, 128)
    rqb[i] = rqs[i]

    d_place().start()
    d_new().start()
    over(N_TP - 1, lambda n: d_rq(tp_peer(n), i).start())
    d_place().wait_recv()
    sel[...] = jnp.where(iota((256, 128), 0) == place_r[0:1, :], 1.0, 0.0).astype(BF)
    sel16 = jnp.where(iota((16, 8), 0) == place_r[4:5, 0:8], 1.0, 0.0)

    def pack(p):
        h = head(p)
        d_stage1(h, 0).wait_recv()
        d_stage1(h, 1).wait_recv()
        x = land[h].reshape(128, 2 * HD)
        y = jnp.dot(sel[...], x, preferred_element_type=F32).astype(BF)
        pk[h] = y.reshape(8, 32, 2 * HD)
        over(N_GRP - 1, lambda k: d_kv_y(h, grp_peer(k), g).start())
        kvb[h, g] = pk[h, g]

        @pl.when(p + AHEAD < KVH)
        def _():
            start1(p + AHEAD)

        @pl.when((p >= Q_FROM) & (p < Q_FROM + 4))
        def _():
            start_q(p - Q_FROM)

    def pack_new():
        d_new().wait_recv()
        new = new_r[...].astype(F32)
        for c in range(16):
            cols = slice(128 * c, 128 * c + 128)
            y = jnp.dot(sel16, new[8 * c:8 * c + 8], preferred_element_type=F32).astype(BF)
            npk[:, :, cols] = y.reshape(8, 2, 128)
        over(N_GRP - 1, lambda k: d_new_y(grp_peer(k), g).start())
        nb[g] = npk[g]

    rrow, rcol = iota((32, 512), 0) % 2, iota((32, 512), 1)
    length = jnp.where(rrow == 0, len_s[0], len_s[1])
    rvalid = (rcol // 256 == rrow) & (rcol % 256 < length)
    first = iota((32, 128), 0) % 2 == 0

    def resident(h):
        q = jnp.concatenate([rqb[2 * h], rqb[2 * h + 1]], axis=0)
        kcols = pl.ds(pl.multiple_of(h * 128, 128), 128)
        vcols = pl.ds(pl.multiple_of(KVH * HD + h * 128, 128), 128)
        k = rkv[:, :, kcols].reshape(512, 128)
        v = rkv[:, :, vcols].reshape(512, 128)
        nk = rn_v[:, kcols].astype(F32)
        nv = rn_v[:, vcols].astype(F32)
        o = attend(
            q, k, v, jnp.where(first, nk[0:1], nk[1:2]), jnp.where(first, nv[0:1], nv[1:2]), rvalid
        )
        ros[2 * h] = o[0:16]
        ros[2 * h + 1] = o[16:32]

    def resident_all():
        l_kv().wait()
        all_tp(rqs, rqb, rqss, rqr).wait_recv()
        over(KVH, resident)
        over(N_TP - 1, lambda k: d_ro(tp_peer(k), i).start())
        rob[i] = ros[i]

    hvalid = iota((256, 256), 0) % 16 == iota((256, 256), 1) // 16

    def handed(p):
        h = head(p)
        all_kv_y(h).wait_recv()
        for t2 in range(2):
            @pl.when(2 * h + t2 != i)
            def _():
                d_q(2 * h + t2, 2 * h + t2).wait_recv()
        q = jnp.concatenate(
            [
                qb[2 * h + t2, :, :, 128 * j:128 * j + 128].reshape(16, 128)
                for t2 in range(2) for j in range(8)
            ],
            axis=0,
        )
        k = kvb[h, :, :, 0:128].reshape(256, 128)
        v = kvb[h, :, :, 128:256].reshape(256, 128)
        kcols = pl.ds(pl.multiple_of(h * 128, 128), 128)
        vcols = pl.ds(pl.multiple_of(KVH * HD + h * 128, 128), 128)
        nk = nb[:, :, kcols].reshape(16, 128).astype(F32)
        nv = nb[:, :, vcols].reshape(16, 128).astype(F32)
        o = attend(q, k, v, jnp.tile(nk, (16, 1)), jnp.tile(nv, (16, 1)), hvalid)
        for t2 in range(2):
            for j in range(8):
                at = 16 * (8 * t2 + j)
                osd[2 * h + t2, :, :, 128 * j:128 * j + 128] = o[at:at + 16].reshape(8, 2, 128)
        for t2 in range(2):
            @pl.when(2 * h + t2 != i)
            def _():
                d_out(2 * h + t2, i).start()

    span(0, LAG, pack)
    pack_new()
    all_new_y().wait_recv()
    l_q().wait()

    def both(p):
        pack(p)
        handed(p - LAG)

    span(LAG, RESIDENT_AT, both)
    resident_all()
    span(RESIDENT_AT, KVH, both)
    span(KVH - LAG, KVH, handed)
    l_out().start()

    all_tp(ros, rob, rosm, ror).wait_recv()
    rof[...] = rob[...].reshape(256, 128).astype(F32)
    for j in range(8):
        for r in range(2):
            rot[pl.ds(32 * j + r, 16, stride=2), :] = rof[pl.ds(2 * j + r, 16, stride=16), :]
    for j in range(8):
        ro_ref[:, 128 * j:128 * j + 128] = rot[32 * j:32 * j + 32].astype(BF)

    d_place().wait_send()
    d_new().wait_send()

    def end_kv(h):
        d_stage1(h, 0).wait_send()
        d_stage1(h, 1).wait_send()

    over(KVH, end_kv)
    all_kv_sent().wait_send()
    all_new_y().wait_send()
    all_tp(rqs, rqb, rqss, rqr).wait_send()
    all_tp(hq_any, qb, qs, qr.at[i]).wait_send()
    all_tp(ros, rob, rosm, ror).wait_send()
    all_tp(osd, ho_ref, os_, orr).wait_send()
    all_tp(osd, ho_ref, os_, orr).wait_recv()
    l_out().wait()


def write_kernel(ro, ho, kvb, ro_o, ho_o, hc_o, sems):
    copies = [
        pltpu.make_async_copy(ro, ro_o, sems.at[0]),
        pltpu.make_async_copy(ho, ho_o, sems.at[1]),
    ]
    for h in range(KVH):
        for part in range(2):
            copies.append(pltpu.make_async_copy(
                kvb.at[h, :, :, pl.ds(part * HD, HD)],
                hc_o.at[:, :, pl.ds((part * KVH + h) * HD, HD)],
                sems.at[2 + 2 * h + part],
            ))
    for copy in copies:
        copy.start()
    for copy in copies:
        copy.wait()


def body(
    resident_kv, resident_query, resident_new, lengths, fresh_kv, handed_query, fresh_new, matching
):
    vm = pl.BlockSpec(memory_space=pltpu.VMEM)
    hbm = pl.BlockSpec(memory_space=pltpu.HBM)
    dma = pltpu.SemaphoreType.DMA
    results = (
        jax.ShapeDtypeStruct((32, 1024), BF),
        jax.ShapeDtypeStruct((16, 8, 2, 1024), BF),
    )
    ro, ho, kvb = pl.pallas_call(
        kernel,
        out_shape=results + (jax.ShapeDtypeStruct((KVH, 8, 32, 2 * HD), BF),),
        in_specs=[hbm] * 8,
        out_specs=(vm, vm, vm),
        scratch_shapes=[
            pltpu.VMEM((32, 1024), BF),
            pltpu.VMEM((2, 2048), BF),
            pltpu.SMEM((2,), jnp.int32),
            pltpu.VMEM((8, 2048), BF),
            pltpu.VMEM((1, 8), jnp.int32),
            pltpu.VMEM((2, 256, 2048), BF),
            pltpu.VMEM((256, 128), F32),
            pltpu.VMEM((256, 128), F32),
            pltpu.VMEM((16, 16, 128), BF),
            pltpu.VMEM((16, 16, 128), BF),
            pltpu.VMEM((16, 16, 128), BF),
            pltpu.VMEM((16, 16, 128), BF),
            pltpu.VMEM((256, 128), F32),
            pltpu.VMEM((256, 128), F32),
            pltpu.VMEM((8, 128), jnp.int32),
            pltpu.VMEM((8, 128), jnp.int32),
            pltpu.VMEM((128, 128), BF),
            pltpu.VMEM((128, 128), BF),
            pltpu.VMEM((8, 2, 2048), BF),
            pltpu.VMEM((8, 2, 2048), BF),
            pltpu.VMEM((KVH, 8, 16, 2 * HD), BF),
            pltpu.VMEM((256, 128), BF),
            pltpu.VMEM((KVH, 8, 32, 2 * HD), BF),
            pltpu.VMEM((16, 8, 2, 1024), BF),
            pltpu.VMEM((16, 8, 2, 1024), BF),
            dma((8,)),
            dma, dma, dma, dma,
            dma((KVH, 2)), dma((KVH, 2)),
            dma, dma,
            dma, dma((KVH,)),
            dma, dma, dma, dma((16,)),
            dma, dma, dma, dma,
        ],
        compiler_params=pltpu.CompilerParams(
            collective_id=0, has_side_effects=True, vmem_limit_bytes=40 * 1024 * 1024
        ),
        name="handoff",
    )(*(
        pltpu.with_memory_space_constraint(array, pltpu.HBM)
        for array in (
            resident_kv, resident_query, resident_new, lengths, fresh_kv,
            handed_query.reshape(16, 8, 2, 1024), fresh_new, matching.reshape(1, 8),
        )
    ))
    ro, ho, hc = pl.pallas_call(
        write_kernel,
        out_shape=results + (jax.ShapeDtypeStruct((8, 32, 2048), BF),),
        in_specs=[vm] * 3,
        out_specs=(hbm, hbm, hbm),
        scratch_shapes=[dma((2 + 2 * KVH,))],
        compiler_params=pltpu.CompilerParams(vmem_limit_bytes=4 * 1024 * 1024),
        name="write",
    )(*(pltpu.with_memory_space_constraint(array, pltpu.VMEM) for array in (ro, ho, kvb)))
    return (
        ro,
        ho.reshape(1, 16, 8, 2, 1024),
        hc.reshape(1, 1, 8, 2, 16, 2048),
    )


def solution(mesh):
    return jax.shard_map(
        body,
        mesh=mesh,
        in_specs=(
            P(("side", "grp", "tp"), None, None),
            P(("side", "grp"), "tp"),
            P(("side", "grp", "tp"), None),
            P(("side", "grp", "tp")),
            P(("side", "grp", "tp"), None, None),
            P(("side", "grp"), None, None, None, "tp"),
            P(("side", "grp", "tp"), None),
            P(("side", "grp", "tp"), None),
        ),
        out_specs=(
            P(("side", "grp"), "tp"),
            P(("side", "grp"), None, None, None, "tp"),
            P(("side", "grp"), "tp", None, None, None, None),
        ),
        check_vma=False,
    )
```

```python
import math

import jax
import jax.numpy as jnp
from jax import lax
from jax.experimental import pallas as pl
from jax.experimental.pallas import tpu as pltpu
from jax.sharding import PartitionSpec as P

MESH = pl.DeviceIdType.MESH
BF = jnp.bfloat16
F32 = jnp.float32
HD = 128
KVH = 8
N_GRP = 8
N_TP = 16
NEG_FILL = -1e30
SCALE = 1.0 / math.sqrt(HD)
LAG = 3
AHEAD = 4
RESIDENT_AT = 5
Q_FROM = 0


def iota(shape, dim):
    return lax.broadcasted_iota(jnp.int32, shape, dim)


def attend(q, k, v, new_k, new_v, valid):
    s = lax.dot_general(q, k, (((1,), (1,)), ((), ())), preferred_element_type=F32) * SCALE
    s = jnp.where(valid, s, NEG_FILL)
    sn = jnp.sum(q.astype(F32) * new_k, axis=-1, keepdims=True) * SCALE
    top = jnp.maximum(jnp.max(s, axis=-1, keepdims=True), sn)
    p = jnp.exp(s - top)
    pn = jnp.exp(sn - top)
    total = jnp.sum(p, axis=-1, keepdims=True) + pn
    numer = jnp.dot(p.astype(BF), v, preferred_element_type=F32)
    numer = numer + pn.astype(BF).astype(F32) * new_v
    return (numer / total).astype(BF)


def kernel(
    kv_any, rq_any, rn_any, len_any, fkv_any, hq_any, fn_any, mt_any,
    ro_ref, ho_ref, kvb,
    rq_v, rn_v, len_s, fn_v, mt_v,
    rkv, rqf, rqt, rqs, rqb, ros, rob, rof, rot, place_s, place_r, new_s, new_r,
    npk, nb, land, sel, pk, qb, osd,
    loc, pls, plr, nws, nwr, s1s, s1r, nys, nyr, s2s, s2r, rqss, rqr, qs, qr, rosm, ror, os_, orr,
):
    side = lax.axis_index("side")
    g = lax.axis_index("grp")
    i = lax.axis_index("tp")
    sp = (side + 2) % 4
    x, zh = i // 4, i % 4

    def head(p):
        alternate = side % 2
        step = p + alternate * (p // 2 - p)
        odd = p // 4 + alternate * (p % 2 - p // 4)
        return 2 * ((x + step) % 4) + odd

    def remote(src, dst, ss, rs, **dev):
        return pltpu.make_async_remote_copy(
            src_ref=src, dst_ref=dst, send_sem=ss, recv_sem=rs, device_id=dev, device_id_type=MESH
        )

    def span(low, high, f):
        def body(k, _):
            f(k)
            return 0

        lax.fori_loop(low, high, body, 0)

    def over(n, f):
        def body(k, _):
            f(k)
            return 0

        lax.fori_loop(0, n, body, 0)

    def d_stage1(h, part):
        cols = pl.ds(pl.multiple_of(part * KVH * HD + h * HD, 128), HD)
        return remote(
            fkv_any.at[:, :, cols], land.at[h, :, :, pl.ds(part * HD, HD)],
            s1s.at[h, part], s1r.at[h, part], side=sp,
        )

    def d_place():
        return remote(place_s, place_r, pls, plr, side=sp)

    def d_new():
        return remote(new_s, new_r, nws, nwr, side=sp)

    def d_new_y(d, me):
        return remote(npk.at[d], nb.at[me], nys, nyr, grp=d)

    def d_kv_y(c, d, me):
        return remote(pk.at[c, d], kvb.at[c, me], s2s, s2r.at[c], grp=d)

    def d_rq(t, me):
        return remote(rqs.at[t], rqb.at[me], rqss, rqr, tp=t)

    def d_q(t, me):
        return remote(hq_any.at[t], qb.at[me], qs, qr.at[me], tp=t)

    def d_ro(t, me):
        return remote(ros.at[t], rob.at[me], rosm, ror, tp=t)

    def d_out(t, me):
        return remote(osd.at[t], ho_ref.at[me], os_, orr, tp=t)

    def all_new_y():
        return remote(npk.at[pl.ds(0, 7)], nb.at[pl.ds(0, 7)], nys, nyr, grp=g)

    def all_kv_y(c):
        return remote(pk.at[c, pl.ds(0, 7)], kvb.at[c, pl.ds(0, 7)], s2s, s2r.at[c], grp=g)

    def all_kv_sent():
        return remote(pk.at[pl.ds(0, 7)], kvb.at[pl.ds(0, 7)], s2s, s2r.at[0], grp=g)

    def all_tp(src, dst, ss, rs):
        return remote(src.at[pl.ds(0, 15)], dst.at[pl.ds(0, 15)], ss, rs, tp=i)

    def local(src, dst, at):
        return pltpu.make_async_copy(src, dst, loc.at[at])

    def l_kv():
        return local(kv_any, rkv, 0)

    def l_q():
        return local(hq_any.at[i], qb.at[i], 1)

    def l_out():
        return local(osd.at[i], ho_ref.at[i], 2)

    small = [
        local(mt_any, mt_v, 3), local(rq_any, rq_v, 4), local(fn_any, fn_v, 5),
        local(rn_any, rn_v, 6), local(len_any, len_s, 7),
    ]

    def tp_peer(k):
        return (i + N_TP - 1 - k) % N_TP

    def grp_peer(k):
        return (g + 1 + k) % N_GRP

    barrier = pltpu.get_barrier_semaphore()
    over(N_TP - 1, lambda k: pl.semaphore_signal(
        barrier, inc=1, device_id={"tp": tp_peer(k)}, device_id_type=MESH))
    over(N_GRP - 1, lambda k: pl.semaphore_signal(
        barrier, inc=1, device_id={"grp": grp_peer(k)}, device_id_type=MESH))
    pl.semaphore_signal(barrier, inc=1, device_id={"side": sp}, device_id_type=MESH)
    for copy in small:
        copy.start()
    l_q().start()
    l_kv().start()
    def start1(p):
        d_stage1(head(p), 0).start()
        d_stage1(head(p), 1).start()

    def start_q(n):
        def one(dz):
            t = (x + 4 - n) % 4 * 4 + (zh + dz) % 4

            @pl.when(t != i)
            def _():
                d_q(t, i).start()

        over(4, one)

    pl.semaphore_wait(barrier, N_TP + N_GRP - 1)

    span(0, AHEAD, start1)
    for copy in small:
        copy.wait()

    row, lane = iota((8, 128), 0), iota((8, 128), 1)
    across = jnp.broadcast_to(mt_v[...], (8, 8))
    down = jnp.sum(jnp.where(iota((8, 8), 0) == iota((8, 8), 1), across, 0), axis=1, keepdims=True)
    m = jnp.broadcast_to(down, (8, 128))

    def places(req):
        mrow = jnp.sum(jnp.where(row == req, m, 0), axis=0, keepdims=True)
        mine = jnp.broadcast_to(mrow, (8, 128))
        rank = jnp.sum(jnp.where((m == mine) & (row < req), 1, 0), axis=0, keepdims=True)
        return jnp.broadcast_to(mrow * 2 + rank, (8, 128))

    wide = places(lane // 16) * 16 + lane % 16
    narrow = jnp.where(lane < 8, places(lane), -1)
    place_s[...] = jnp.where(row < 4, wide, narrow)
    d_place().start()
    new_s[...] = jnp.concatenate(
        [fn_v[:, 128 * c:128 * c + 128].astype(F32) for c in range(16)], axis=0
    ).astype(BF)
    d_new().start()
    for j in range(8):
        rqf[32 * j:32 * j + 32] = rq_v[:, 128 * j:128 * j + 128].astype(F32)
    for j in range(8):
        for r in range(2):
            rqt[pl.ds(2 * j + r, 16, stride=16), :] = rqf[pl.ds(32 * j + r, 16, stride=2), :]
    rqs[...] = rqt[...].astype(BF).reshape(16, 16, 128)
    rqb[i] = rqs[i]

    over(N_TP - 1, lambda n: d_rq(tp_peer(n), i).start())
    d_place().wait_recv()
    sel[...] = jnp.where(iota((256, 128), 0) == place_r[0:1, :], 1.0, 0.0).astype(BF)
    sel16 = jnp.where(iota((16, 8), 0) == place_r[4:5, 0:8], 1.0, 0.0)

    def pack(p):
        h = head(p)
        d_stage1(h, 0).wait_recv()
        d_stage1(h, 1).wait_recv()
        x = land[h].reshape(128, 2 * HD)
        y = jnp.dot(sel[...], x, preferred_element_type=F32).astype(BF)
        pk[h] = y.reshape(8, 32, 2 * HD)
        over(N_GRP - 1, lambda k: d_kv_y(h, grp_peer(k), g).start())
        kvb[h, g] = pk[h, g]

        @pl.when(p + AHEAD < KVH)
        def _():
            start1(p + AHEAD)

        @pl.when((p >= Q_FROM) & (p < Q_FROM + 4))
        def _():
            start_q(p - Q_FROM)

    def pack_new():
        d_new().wait_recv()
        new = new_r[...].astype(F32)
        for c in range(16):
            cols = slice(128 * c, 128 * c + 128)
            y = jnp.dot(sel16, new[8 * c:8 * c + 8], preferred_element_type=F32).astype(BF)
            npk[:, :, cols] = y.reshape(8, 2, 128)
        over(N_GRP - 1, lambda k: d_new_y(grp_peer(k), g).start())
        nb[g] = npk[g]

    rrow, rcol = iota((32, 512), 0) % 2, iota((32, 512), 1)
    length = jnp.where(rrow == 0, len_s[0], len_s[1])
    rvalid = (rcol // 256 == rrow) & (rcol % 256 < length)
    first = iota((32, 128), 0) % 2 == 0

    def resident(h):
        q = jnp.concatenate([rqb[2 * h], rqb[2 * h + 1]], axis=0)
        kcols = pl.ds(pl.multiple_of(h * 128, 128), 128)
        vcols = pl.ds(pl.multiple_of(KVH * HD + h * 128, 128), 128)
        k = rkv[:, :, kcols].reshape(512, 128)
        v = rkv[:, :, vcols].reshape(512, 128)
        nk = rn_v[:, kcols].astype(F32)
        nv = rn_v[:, vcols].astype(F32)
        o = attend(
            q, k, v, jnp.where(first, nk[0:1], nk[1:2]), jnp.where(first, nv[0:1], nv[1:2]), rvalid
        )
        ros[2 * h] = o[0:16]
        ros[2 * h + 1] = o[16:32]

    def resident_all():
        l_kv().wait()
        all_tp(rqs, rqb, rqss, rqr).wait_recv()
        over(KVH, resident)
        over(N_TP - 1, lambda k: d_ro(tp_peer(k), i).start())
        rob[i] = ros[i]

    hvalid = iota((256, 256), 0) % 16 == iota((256, 256), 1) // 16

    def handed(p):
        h = head(p)
        all_kv_y(h).wait_recv()
        for t2 in range(2):
            @pl.when(2 * h + t2 != i)
            def _():
                d_q(2 * h + t2, 2 * h + t2).wait_recv()
        q = jnp.concatenate(
            [
                qb[2 * h + t2, :, :, 128 * j:128 * j + 128].reshape(16, 128)
                for t2 in range(2) for j in range(8)
            ],
            axis=0,
        )
        k = kvb[h, :, :, 0:128].reshape(256, 128)
        v = kvb[h, :, :, 128:256].reshape(256, 128)
        kcols = pl.ds(pl.multiple_of(h * 128, 128), 128)
        vcols = pl.ds(pl.multiple_of(KVH * HD + h * 128, 128), 128)
        nk = nb[:, :, kcols].reshape(16, 128).astype(F32)
        nv = nb[:, :, vcols].reshape(16, 128).astype(F32)
        o = attend(q, k, v, jnp.tile(nk, (16, 1)), jnp.tile(nv, (16, 1)), hvalid)
        for t2 in range(2):
            for j in range(8):
                at = 16 * (8 * t2 + j)
                osd[2 * h + t2, :, :, 128 * j:128 * j + 128] = o[at:at + 16].reshape(8, 2, 128)
        for t2 in range(2):
            @pl.when(2 * h + t2 != i)
            def _():
                d_out(2 * h + t2, i).start()

    span(0, LAG, pack)
    pack_new()
    all_new_y().wait_recv()
    l_q().wait()

    def both(p):
        pack(p)
        handed(p - LAG)

    span(LAG, RESIDENT_AT, both)
    resident_all()
    span(RESIDENT_AT, KVH, both)
    span(KVH - LAG, KVH, handed)
    l_out().start()

    all_tp(ros, rob, rosm, ror).wait_recv()
    rof[...] = rob[...].reshape(256, 128).astype(F32)
    for j in range(8):
        for r in range(2):
            rot[pl.ds(32 * j + r, 16, stride=2), :] = rof[pl.ds(2 * j + r, 16, stride=16), :]
    for j in range(8):
        ro_ref[:, 128 * j:128 * j + 128] = rot[32 * j:32 * j + 32].astype(BF)

    d_place().wait_send()
    d_new().wait_send()

    def end_kv(h):
        d_stage1(h, 0).wait_send()
        d_stage1(h, 1).wait_send()

    over(KVH, end_kv)
    all_kv_sent().wait_send()
    all_new_y().wait_send()
    all_tp(rqs, rqb, rqss, rqr).wait_send()
    all_tp(hq_any, qb, qs, qr.at[i]).wait_send()
    all_tp(ros, rob, rosm, ror).wait_send()
    all_tp(osd, ho_ref, os_, orr).wait_send()
    all_tp(osd, ho_ref, os_, orr).wait_recv()
    l_out().wait()


def write_kernel(ro, ho, kvb, ro_o, ho_o, hc_o, sems):
    copies = [
        pltpu.make_async_copy(ro, ro_o, sems.at[0]),
        pltpu.make_async_copy(ho, ho_o, sems.at[1]),
    ]
    for h in range(KVH):
        for part in range(2):
            copies.append(pltpu.make_async_copy(
                kvb.at[h, :, :, pl.ds(part * HD, HD)],
                hc_o.at[:, :, pl.ds((part * KVH + h) * HD, HD)],
                sems.at[2 + 2 * h + part],
            ))
    for copy in copies:
        copy.start()
    for copy in copies:
        copy.wait()


def body(
    resident_kv, resident_query, resident_new, lengths, fresh_kv, handed_query, fresh_new, matching
):
    vm = pl.BlockSpec(memory_space=pltpu.VMEM)
    hbm = pl.BlockSpec(memory_space=pltpu.HBM)
    dma = pltpu.SemaphoreType.DMA
    results = (
        jax.ShapeDtypeStruct((32, 1024), BF),
        jax.ShapeDtypeStruct((16, 8, 2, 1024), BF),
    )
    ro, ho, kvb = pl.pallas_call(
        kernel,
        out_shape=results + (jax.ShapeDtypeStruct((KVH, 8, 32, 2 * HD), BF),),
        in_specs=[hbm] * 8,
        out_specs=(vm, vm, vm),
        scratch_shapes=[
            pltpu.VMEM((32, 1024), BF),
            pltpu.VMEM((2, 2048), BF),
            pltpu.SMEM((2,), jnp.int32),
            pltpu.VMEM((8, 2048), BF),
            pltpu.VMEM((1, 8), jnp.int32),
            pltpu.VMEM((2, 256, 2048), BF),
            pltpu.VMEM((256, 128), F32),
            pltpu.VMEM((256, 128), F32),
            pltpu.VMEM((16, 16, 128), BF),
            pltpu.VMEM((16, 16, 128), BF),
            pltpu.VMEM((16, 16, 128), BF),
            pltpu.VMEM((16, 16, 128), BF),
            pltpu.VMEM((256, 128), F32),
            pltpu.VMEM((256, 128), F32),
            pltpu.VMEM((8, 128), jnp.int32),
            pltpu.VMEM((8, 128), jnp.int32),
            pltpu.VMEM((128, 128), BF),
            pltpu.VMEM((128, 128), BF),
            pltpu.VMEM((8, 2, 2048), BF),
            pltpu.VMEM((8, 2, 2048), BF),
            pltpu.VMEM((KVH, 8, 16, 2 * HD), BF),
            pltpu.VMEM((256, 128), BF),
            pltpu.VMEM((KVH, 8, 32, 2 * HD), BF),
            pltpu.VMEM((16, 8, 2, 1024), BF),
            pltpu.VMEM((16, 8, 2, 1024), BF),
            dma((8,)),
            dma, dma, dma, dma,
            dma((KVH, 2)), dma((KVH, 2)),
            dma, dma,
            dma, dma((KVH,)),
            dma, dma, dma, dma((16,)),
            dma, dma, dma, dma,
        ],
        compiler_params=pltpu.CompilerParams(
            collective_id=0, has_side_effects=True, vmem_limit_bytes=40 * 1024 * 1024
        ),
        name="handoff",
    )(*(
        pltpu.with_memory_space_constraint(array, pltpu.HBM)
        for array in (
            resident_kv, resident_query, resident_new, lengths, fresh_kv,
            handed_query.reshape(16, 8, 2, 1024), fresh_new, matching.reshape(1, 8),
        )
    ))
    ro, ho, hc = pl.pallas_call(
        write_kernel,
        out_shape=results + (jax.ShapeDtypeStruct((8, 32, 2048), BF),),
        in_specs=[vm] * 3,
        out_specs=(hbm, hbm, hbm),
        scratch_shapes=[dma((2 + 2 * KVH,))],
        compiler_params=pltpu.CompilerParams(vmem_limit_bytes=4 * 1024 * 1024),
        name="write",
    )(*(pltpu.with_memory_space_constraint(array, pltpu.VMEM) for array in (ro, ho, kvb)))
    return (
        ro,
        ho.reshape(1, 16, 8, 2, 1024),
        hc.reshape(1, 1, 8, 2, 16, 2048),
    )


def solution(mesh):
    return jax.shard_map(
        body,
        mesh=mesh,
        in_specs=(
            P(("side", "grp", "tp"), None, None),
            P(("side", "grp"), "tp"),
            P(("side", "grp", "tp"), None),
            P(("side", "grp", "tp")),
            P(("side", "grp", "tp"), None, None),
            P(("side", "grp"), None, None, None, "tp"),
            P(("side", "grp", "tp"), None),
            P(("side", "grp", "tp"), None),
        ),
        out_specs=(
            P(("side", "grp"), "tp"),
            P(("side", "grp"), None, None, None, "tp"),
            P(("side", "grp"), "tp", None, None, None, None),
        ),
        check_vma=False,
    )
```
